1024 devices in a mesh: blk: 64 (over z_lo, x, core), group: 16 (over y, z_hi).
Axes of the slice: x: 4, y: 4, z: 32 (z_hi: 4, z_lo: 8; z = z_hi * 8 + z_lo), core: 2. Of those that a mesh axis runs over, the one named last changes fastest.
Arguments:
- image_feats: bfloat16 [131072, 1152], P(('blk', 'group')), may hold values from -0.19921875 to 0.19921875
- text_feats: bfloat16 [131072, 1152], P(('blk', 'group')), may hold values from -0.19921875 to 0.19921875
- positive: int32 [1024, 128], P(('blk', 'group')), may hold values from 0 to 127, each once within a row
- scale: float32 [1], replicated, may hold values from 5 to 20
- bias: float32 [1], replicated, may hold values from -4 to -1
Outputs:
- loss_rows: float32 [131072], P(('blk', 'group'))
- image_grad: float32 [131072, 1152], P(('blk', 'group'))
- text_grad: float32 [131072, 1152], P(('blk', 'group'))
The draws below stay inside these ranges and needn't reach their ends.
Inputs may be any that keep to these rules, and one draw needn't show every extreme that they name: Each row of positive is a permutation of 0 to 127.
All inputs are finite; a program needn't handle non-finite values.
Results may differ from the reference program's by a relative error of at most 0.0041.
Values may be sent and summed in bfloat16 or wider, within the bound.
No kernel may reach another device: no remote copies, remote signals or barrier semaphores. Data moves between devices by JAX's collectives and lax.ppermute only.
A program may use at most 32 MiB of HBM per device.

```python
import math
import jax
import jax.numpy as jnp
from jax import lax

D = 1152
ROWS = 128
SPAN = 8
BLOCKS = 1024
BATCH = 131072
N_BLK = 64
N_GROUP = 16


def steps_of(key, dims, split, least, high):
    level = 1.0
    for dim, blocks in split:
        steps = jax.random.uniform(jax.random.fold_in(jax.random.fold_in(key, 6), dim), (blocks,), jnp.float32, least / len(split), high / len(split))
        level = level * jnp.repeat(jnp.exp(steps), dims[dim] // blocks).reshape((-1,) + (1,) * (len(dims) - 1 - dim))
    return level


def bell_draw(stream_key, dims, deviation, reach, pieces=(), kind=jnp.bfloat16):
    level = steps_of(stream_key, dims, pieces, -0.22, 0.18) if pieces else 1.0
    values = jax.random.normal(stream_key, dims, jnp.float32) * deviation * level
    return jnp.minimum(jnp.maximum(values, -reach), reach).astype(kind)


def setup_inputs(seed: int = 0) -> dict:
    seeds = jax.random.split(jax.random.key(seed), 6)
    return {
        "image_feats": bell_draw(seeds[0], (BATCH, D), 0.03, 0.19921875, ((0, 1024),)),
        "text_feats": bell_draw(seeds[1], (BATCH, D), 0.03, 0.19921875, ((0, 1024),)),
        "positive": jax.vmap(lambda own: jax.random.permutation(own, ROWS))(jax.random.split(seeds[2], BLOCKS)).reshape((BLOCKS, ROWS)).astype(jnp.int32),
        "scale": jnp.clip(jnp.exp(jax.random.uniform(seeds[3], (1,), jnp.float32, math.log(5.0), math.log(20.0))), 5.0, 20.0),
        "bias": jnp.clip(jax.random.uniform(seeds[4], (1,), jnp.float32, -4.0, -1.0), -4.0, -1.0),
    }


def normalize(values):
    floats = values.astype(jnp.float32)
    inverse = lax.rsqrt(lax.optimization_barrier(jnp.sum(floats * floats, axis=-1, keepdims=True)) + 1e-06)
    return (floats * inverse, inverse)

def pair_terms(logit, sign):
    return (jax.nn.softplus(-sign * logit), -sign * jax.nn.sigmoid(-sign * logit))

def reference(image_feats, text_feats, positive, scale, bias):
    tau = scale[0]
    offset = bias[0]
    x_norm, x_inv = normalize(image_feats)
    y_norm, y_inv = normalize(text_feats)
    x_blocks = x_norm.astype(jnp.bfloat16).reshape(N_BLK, N_GROUP, ROWS, D)
    y_blocks = y_norm.astype(jnp.bfloat16).reshape(N_BLK, N_GROUP, ROWS, D)
    x_floats = x_blocks.astype(jnp.float32)
    equal = positive.reshape(N_BLK, N_GROUP, ROWS)[..., None] == jnp.arange(ROWS, dtype=jnp.int32)
    own_sign = jnp.where(equal, 1.0, -1.0).astype(jnp.float32)
    loss_sum = jnp.zeros((N_BLK, N_GROUP, ROWS), jnp.float32)
    grad_x = jnp.zeros((N_BLK, N_GROUP, ROWS, D), jnp.float32)
    grad_y = jnp.zeros((N_BLK, N_GROUP, ROWS, D), jnp.float32)
    for step in range(SPAN + 1):
        if step < SPAN:
            other = jnp.roll(y_blocks, step, axis=0)
        else:
            other = jnp.roll(y_blocks, 1, axis=1)
        sign = own_sign if step == 0 else jnp.float32(-1.0)
        other_f = other.astype(jnp.float32)
        logit = tau * jnp.einsum('bgrd,bgcd->bgrc', x_floats, other_f) + offset
        loss, slope = pair_terms(logit, sign)
        loss_sum = loss_sum + lax.optimization_barrier(jnp.sum(loss, axis=-1))
        slope_f = lax.optimization_barrier(slope.astype(jnp.bfloat16)).astype(jnp.float32)
        grad_x = grad_x + tau * jnp.einsum('bgrc,bgcd->bgrd', slope_f, other_f)
        term = jnp.einsum('bgrc,bgrd->bgcd', slope_f, x_floats)
        if step < SPAN:
            grad_y = grad_y + tau * jnp.roll(term, -step, axis=0)
        else:
            grad_y = grad_y + tau * jnp.roll(term, -1, axis=1)
    grad_x = grad_x.reshape(BATCH, D)
    grad_y = grad_y.reshape(BATCH, D)
    image_grad = (grad_x - x_norm * lax.optimization_barrier(jnp.sum(x_norm * grad_x, axis=-1, keepdims=True))) * x_inv
    text_grad = (grad_y - y_norm * lax.optimization_barrier(jnp.sum(y_norm * grad_y, axis=-1, keepdims=True))) * y_inv
    loss_rows = loss_sum.reshape(BATCH) / jnp.float32((SPAN + 1) * ROWS)
    return (loss_rows, image_grad, text_grad)
```

```python
import functools

import jax
import jax.numpy as jnp
from jax import lax
from jax.experimental import pallas as pl
from jax.experimental.pallas import tpu as pltpu
from jax.sharding import PartitionSpec as P

SPAN = 8
CORES = 2
CHIPS = SPAN // CORES
F32 = jnp.float32
BF16 = jnp.bfloat16


def shifted(x, axis, by):
    size = lax.axis_size(axis)
    return lax.ppermute(x, axis, [(i, (i + by) % size) for i in range(size)])


def in_row(x, by):
    pairs = []
    for i in range(lax.axis_size("blk")):
        first, place = i - i % SPAN, i % SPAN
        pairs.append((i, first + (place + CORES * by) % SPAN))
    return lax.ppermute(x, "blk", pairs)


def to_twin(x):
    return lax.ppermute(x, "blk", [(i, i ^ 1) for i in range(lax.axis_size("blk"))])


def row_inverse(values):
    floats = values.astype(F32)
    return lax.rsqrt(jnp.sum(floats * floats, axis=-1, keepdims=True) + 1e-06)


def along_lanes(column):
    rows = column.shape[0]
    return jnp.broadcast_to(column, (rows, rows)).T


def by_rows(left, right):
    return lax.dot_general(left, right, (((1,), (1,)), ((), ())), preferred_element_type=F32)


def by_cols(left, right):
    return lax.dot_general(left, right, (((0,), (0,)), ((), ())), preferred_element_type=F32)


def product(left, right):
    return jnp.dot(left, right, preferred_element_type=F32)


def loss_and_slope(u):
    small = jnp.exp(-jnp.abs(u))
    whole = 1.0 + small
    return (
        jnp.maximum(u, 0.0) + jnp.log1p(small),
        jnp.where(u >= 0.0, 1.0, small) / whole,
    )


def inner_kernel(scale, bias, x_ref, y_ref, pos_ref, *rest):
    pairs, (loss_ref, gx_ref, gy_ref) = rest[:-3], rest[-3:]
    tau, offset = scale[0], bias[0]
    rows = x_ref.shape[0]
    x, y = x_ref[...], y_ref[...]
    x_inv, y_inv = row_inverse(x), row_inverse(y)
    x_tau, y_tau = x_inv * tau, y_inv * tau
    y_lanes = along_lanes(y_inv)
    own = by_rows(x, y) * x_tau * y_lanes + offset
    place = lax.broadcasted_iota(jnp.int32, (rows, rows), 1)
    equal = pos_ref[...] == place
    away = jnp.where(equal, -1.0, 1.0)
    loss, slope = loss_and_slope(away * own)
    slope = slope * away
    gx = product((slope * y_lanes).astype(BF16), y)
    gy = by_cols((slope * x_inv).astype(BF16), x)
    for ref in pairs:
        other = ref[:rows, :]
        lanes = along_lanes(row_inverse(other))
        add, slope = loss_and_slope(by_rows(x, other) * x_tau * lanes + offset)
        loss = loss + add
        gx = gx + product((slope * lanes).astype(BF16), other)
        other = ref[rows:, :]
        lanes = along_lanes(row_inverse(other))
        _, slope = loss_and_slope(by_rows(y, other) * y_tau * lanes + offset)
        gy = gy + product((slope * lanes).astype(BF16), other)
    loss_ref[...] = loss
    gx_ref[...] = gx
    gy_ref[...] = gy


def outer_kernel(scale, bias, x_ref, y_ref, yg_ref, xg_ref, loss_in, gx_in, gy_in, loss_ref, ix_ref, ty_ref):
    tau, offset = scale[0], bias[0]
    rows = x_ref.shape[0]
    x, y = x_ref[...], y_ref[...]
    x_inv, y_inv = row_inverse(x), row_inverse(y)
    other = yg_ref[...]
    lanes = along_lanes(row_inverse(other))
    add, slope = loss_and_slope(by_rows(x, other) * (x_inv * tau) * lanes + offset)
    loss_ref[...] = jnp.sum((loss_in[...] + add).T, axis=0, keepdims=True) / F32((SPAN + 1) * rows)
    gx = (gx_in[...] + product((slope * lanes).astype(BF16), other)) * tau
    xn = x.astype(F32) * x_inv
    ix_ref[...] = (gx - xn * jnp.sum(xn * gx, axis=-1, keepdims=True)) * x_inv
    other = xg_ref[...]
    lanes = along_lanes(row_inverse(other))
    _, slope = loss_and_slope(by_rows(y, other) * (y_inv * tau) * lanes + offset)
    gy = (gy_in[...] + product((slope * lanes).astype(BF16), other)) * tau
    yn = y.astype(F32) * y_inv
    ty_ref[...] = (gy - yn * jnp.sum(yn * gy, axis=-1, keepdims=True)) * y_inv


def call(kernel, outs, flops, scale, bias, *args):
    return pl.pallas_call(
        kernel,
        out_shape=[jax.ShapeDtypeStruct(shape, F32) for shape in outs],
        in_specs=[pl.BlockSpec(memory_space=pltpu.SMEM)] * 2
        + [pl.BlockSpec(memory_space=pltpu.VMEM)] * len(args),
        out_specs=[pl.BlockSpec(memory_space=pltpu.VMEM)] * len(outs),
        compiler_params=pltpu.CompilerParams(vmem_limit_bytes=40 * 1024 * 1024),
        cost_estimate=pl.CostEstimate(flops=flops, bytes_accessed=8 * 1024 * 1024, transcendentals=0),
    )(scale, bias, *args)


def local(image_feats, text_feats, positive, scale, bias):
    x, y = image_feats, text_feats
    rows, width = x.shape
    place = lax.axis_index("blk") % SPAN
    chip, core = place // CORES, place % CORES
    y_back = shifted(y, "blk", SPAN)
    x_next = shifted(x, "blk", -SPAN)
    y_outer = shifted(y, "group", 1)
    x_outer = shifted(x, "group", -1)
    up = jnp.concatenate([y, x_next], axis=0)
    down = jnp.concatenate([y_back, x], axis=0)
    pairs = [in_row(jnp.where(chip + by < CHIPS, up, down), by) for by in range(1, CHIPS)]
    twins = [to_twin(jnp.where(core == 0, up, down))] + [to_twin(pair) for pair in pairs]
    block = (rows, width)
    work = 2 * rows * rows * width
    loss, gx, gy = call(
        inner_kernel, [(rows, rows), block, block], work * 31, scale, bias, x, y,
        positive.reshape(rows, 1), *pairs, *twins,
    )
    loss, image_grad, text_grad = call(
        outer_kernel, [(1, rows), block, block], work * 4, scale, bias, x, y, y_outer, x_outer, loss, gx, gy
    )
    return (loss[0], image_grad, text_grad)


def solution(mesh):
    rows = P(("blk", "group"), None)
    return jax.shard_map(
        local,
        mesh=mesh,
        in_specs=(rows, rows, rows, P(), P()),
        out_specs=(P(("blk", "group")), rows, rows),
        check_vma=False,
    )
```

```python
import functools

import jax
import jax.numpy as jnp
from jax import lax
from jax.experimental import pallas as pl
from jax.experimental.pallas import tpu as pltpu
from jax.sharding import PartitionSpec as P

SPAN = 8
CORES = 2
CHIPS = SPAN // CORES
F32 = jnp.float32
BF16 = jnp.bfloat16


def shifted(x, axis, by):
    size = lax.axis_size(axis)
    return lax.ppermute(x, axis, [(i, (i + by) % size) for i in range(size)])


def in_row(x, by):
    pairs = []
    for i in range(lax.axis_size("blk")):
        first, place = i - i % SPAN, i % SPAN
        pairs.append((i, first + (place + CORES * by) % SPAN))
    return lax.ppermute(x, "blk", pairs)


def to_twin(x):
    return lax.ppermute(x, "blk", [(i, i ^ 1) for i in range(lax.axis_size("blk"))])


def row_inverse(values):
    floats = values.astype(F32)
    return lax.rsqrt(jnp.sum(floats * floats, axis=-1, keepdims=True) + 1e-06)


def along_lanes(column):
    rows = column.shape[0]
    return jnp.broadcast_to(column, (rows, rows)).T


def by_rows(left, right):
    return lax.dot_general(left, right, (((1,), (1,)), ((), ())), preferred_element_type=F32)


def by_cols(left, right):
    return lax.dot_general(left, right, (((0,), (0,)), ((), ())), preferred_element_type=F32)


def product(left, right):
    return jnp.dot(left, right, preferred_element_type=F32)


def loss_and_slope(u):
    small = jnp.exp(-jnp.abs(u))
    whole = 1.0 + small
    return (
        jnp.maximum(u, 0.0) + jnp.log1p(small),
        jnp.where(u >= 0.0, 1.0, small) / whole,
    )


def inner_kernel(scale, bias, x_ref, y_ref, pos_ref, *rest):
    pairs, (loss_ref, gx_ref, gy_ref) = rest[:-3], rest[-3:]
    tau, offset = scale[0], bias[0]
    rows = x_ref.shape[0]
    x, y = x_ref[...], y_ref[...]
    x_inv, y_inv = row_inverse(x), row_inverse(y)
    x_tau, y_tau = x_inv * tau, y_inv * tau
    y_lanes = along_lanes(y_inv)
    own = by_rows(x, y) * x_tau * y_lanes + offset
    place = lax.broadcasted_iota(jnp.int32, (rows, rows), 1).astype(F32)
    match = jnp.broadcast_to(pos_ref[...].astype(F32), (rows, rows)).T
    away = jnp.where(match == place, -1.0, 1.0)
    loss, slope = loss_and_slope(away * own)
    slope = slope * away
    gx = product((slope * y_lanes).astype(BF16), y)
    gy = by_cols((slope * x_inv).astype(BF16), x)
    for ref in pairs:
        other = ref[:rows, :]
        lanes = along_lanes(row_inverse(other))
        add, slope = loss_and_slope(by_rows(x, other) * x_tau * lanes + offset)
        loss = loss + add
        gx = gx + product((slope * lanes).astype(BF16), other)
        other = ref[rows:, :]
        lanes = along_lanes(row_inverse(other))
        _, slope = loss_and_slope(by_rows(y, other) * y_tau * lanes + offset)
        gy = gy + product((slope * lanes).astype(BF16), other)
    loss_ref[...] = loss
    gx_ref[...] = gx
    gy_ref[...] = gy


def outer_kernel(scale, bias, x_ref, y_ref, yg_ref, xg_ref, loss_in, gx_in, gy_in, loss_ref, ix_ref, ty_ref):
    tau, offset = scale[0], bias[0]
    rows = x_ref.shape[0]
    x, y = x_ref[...], y_ref[...]
    x_inv, y_inv = row_inverse(x), row_inverse(y)
    other = yg_ref[...]
    lanes = along_lanes(row_inverse(other))
    add, slope = loss_and_slope(by_rows(x, other) * (x_inv * tau) * lanes + offset)
    loss_ref[...] = jnp.sum((loss_in[...] + add).T, axis=0, keepdims=True) / F32((SPAN + 1) * rows)
    gx = (gx_in[...] + product((slope * lanes).astype(BF16), other)) * tau
    xn = x.astype(F32) * x_inv
    ix_ref[...] = (gx - xn * jnp.sum(xn * gx, axis=-1, keepdims=True)) * x_inv
    other = xg_ref[...]
    lanes = along_lanes(row_inverse(other))
    _, slope = loss_and_slope(by_rows(y, other) * (y_inv * tau) * lanes + offset)
    gy = (gy_in[...] + product((slope * lanes).astype(BF16), other)) * tau
    yn = y.astype(F32) * y_inv
    ty_ref[...] = (gy - yn * jnp.sum(yn * gy, axis=-1, keepdims=True)) * y_inv


def call(kernel, outs, flops, scale, bias, *args):
    return pl.pallas_call(
        kernel,
        out_shape=[jax.ShapeDtypeStruct(shape, F32) for shape in outs],
        in_specs=[pl.BlockSpec(memory_space=pltpu.SMEM)] * 2
        + [pl.BlockSpec(memory_space=pltpu.VMEM)] * len(args),
        out_specs=[pl.BlockSpec(memory_space=pltpu.VMEM)] * len(outs),
        compiler_params=pltpu.CompilerParams(vmem_limit_bytes=40 * 1024 * 1024),
        cost_estimate=pl.CostEstimate(flops=flops, bytes_accessed=8 * 1024 * 1024, transcendentals=0),
    )(scale, bias, *args)


def local(image_feats, text_feats, positive, scale, bias):
    x, y = image_feats, text_feats
    rows, width = x.shape
    place = lax.axis_index("blk") % SPAN
    chip, core = place // CORES, place % CORES
    y_back = shifted(y, "blk", SPAN)
    x_next = shifted(x, "blk", -SPAN)
    y_outer = shifted(y, "group", 1)
    x_outer = shifted(x, "group", -1)
    block = (rows, width)
    work = 2 * rows * rows * width

    def inner(_):
        up = jnp.concatenate([y, x_next], axis=0)
        down = jnp.concatenate([y_back, x], axis=0)
        sends = [jnp.where(chip + by < CHIPS, up, down) for by in range(1, CHIPS)]
        twins = [to_twin(jnp.where(core == 0, up, down))]
        sends[1], twins[0] = lax.optimization_barrier((sends[1], twins[0]))
        pairs = [in_row(sends[by - 1], by) for by in range(1, CHIPS)]
        twins += [to_twin(pair) for pair in pairs]
        loss, gx, gy = call(
            inner_kernel, [(rows, rows), block, block], work * 31, scale, bias, x, y,
            positive, *pairs, *twins,
        )
        return loss, gx, gy

    def skip(_):
        return jnp.zeros((rows, rows), F32), jnp.zeros(block, F32), jnp.zeros(block, F32)

    go = lax.optimization_barrier(jnp.int32(1))
    loss, gx, gy = lax.cond(go > 0, inner, skip, 0)
    loss, image_grad, text_grad = call(
        outer_kernel, [(1, rows), block, block], work * 4, scale, bias, x, y, y_outer, x_outer, loss, gx, gy
    )
    return (loss[0], image_grad, text_grad)


def solution(mesh):
    rows = P(("blk", "group"), None)
    return jax.shard_map(
        local,
        mesh=mesh,
        in_specs=(rows, rows, rows, P(), P()),
        out_specs=(P(("blk", "group")), rows, rows),
        check_vma=False,
    )
```

```python
import functools

import jax
import jax.numpy as jnp
from jax import lax
from jax.experimental import pallas as pl
from jax.experimental.pallas import tpu as pltpu
from jax.sharding import PartitionSpec as P

SPAN = 8
CORES = 2
CHIPS = SPAN // CORES
F32 = jnp.float32
BF16 = jnp.bfloat16


def shifted(x, axis, by):
    size = lax.axis_size(axis)
    return lax.ppermute(x, axis, [(i, (i + by) % size) for i in range(size)])


def in_row(x, by):
    pairs = []
    for i in range(lax.axis_size("blk")):
        first, place = i - i % SPAN, i % SPAN
        pairs.append((i, first + (place + CORES * by) % SPAN))
    return lax.ppermute(x, "blk", pairs)


def next_row(x, by):
    size = lax.axis_size("blk")
    pairs = [(i, i + SPAN * by) for i in range(size) if 0 <= i + SPAN * by < size]
    return lax.ppermute(x, "blk", pairs)


def around(x):
    last = lax.axis_size("blk") - SPAN
    pairs = [(last + i, i) for i in range(SPAN)] + [(i, last + i) for i in range(SPAN)]
    return lax.ppermute(x, "blk", pairs)


def to_twin(x):
    return lax.ppermute(x, "blk", [(i, i ^ 1) for i in range(lax.axis_size("blk"))])


def row_inverse(values):
    floats = values.astype(F32)
    return lax.rsqrt(jnp.sum(floats * floats, axis=-1, keepdims=True) + 1e-06)


def along_lanes(column):
    rows = column.shape[0]
    return jnp.broadcast_to(column, (rows, rows)).T


def by_rows(left, right):
    return lax.dot_general(left, right, (((1,), (1,)), ((), ())), preferred_element_type=F32)


def by_cols(left, right):
    return lax.dot_general(left, right, (((0,), (0,)), ((), ())), preferred_element_type=F32)


def product(left, right):
    return jnp.dot(left, right, preferred_element_type=F32)


def loss_and_slope(u):
    small = jnp.exp(-jnp.abs(u))
    whole = 1.0 + small
    return (
        jnp.maximum(u, 0.0) + jnp.log1p(small),
        jnp.where(u >= 0.0, 1.0, small) / whole,
    )


def inner_kernel(scale, bias, x_ref, y_ref, pos_ref, *rest):
    pairs, (loss_ref, gx_ref, gy_ref) = rest[:-3], rest[-3:]
    tau, offset = scale[0], bias[0]
    rows = x_ref.shape[0]
    x, y = x_ref[...], y_ref[...]
    x_inv, y_inv = row_inverse(x), row_inverse(y)
    x_tau, y_tau = x_inv * tau, y_inv * tau
    y_lanes = along_lanes(y_inv)
    own = by_rows(x, y) * x_tau * y_lanes + offset
    place = lax.broadcasted_iota(jnp.int32, (rows, rows), 1).astype(F32)
    match = jnp.broadcast_to(pos_ref[...].astype(F32), (rows, rows)).T
    away = jnp.where(match == place, -1.0, 1.0)
    loss, slope = loss_and_slope(away * own)
    slope = slope * away
    gx = product((slope * y_lanes).astype(BF16), y)
    gy = by_cols((slope * x_inv).astype(BF16), x)
    for ref in pairs:
        other = ref[:rows, :]
        lanes = along_lanes(row_inverse(other))
        add, slope = loss_and_slope(by_rows(x, other) * x_tau * lanes + offset)
        loss = loss + add
        gx = gx + product((slope * lanes).astype(BF16), other)
        other = ref[rows:, :]
        lanes = along_lanes(row_inverse(other))
        _, slope = loss_and_slope(by_rows(y, other) * y_tau * lanes + offset)
        gy = gy + product((slope * lanes).astype(BF16), other)
    loss_ref[...] = loss
    gx_ref[...] = gx
    gy_ref[...] = gy


def outer_kernel(scale, bias, x_ref, y_ref, yg_ref, xg_ref, loss_in, gx_in, gy_in, loss_ref, ix_ref, ty_ref):
    tau, offset = scale[0], bias[0]
    rows = x_ref.shape[0]
    x, y = x_ref[...], y_ref[...]
    x_inv, y_inv = row_inverse(x), row_inverse(y)
    other = yg_ref[...]
    lanes = along_lanes(row_inverse(other))
    add, slope = loss_and_slope(by_rows(x, other) * (x_inv * tau) * lanes + offset)
    loss_ref[...] = jnp.sum((loss_in[...] + add).T, axis=0, keepdims=True) / F32((SPAN + 1) * rows)
    gx = (gx_in[...] + product((slope * lanes).astype(BF16), other)) * tau
    xn = x.astype(F32) * x_inv
    ix_ref[...] = (gx - xn * jnp.sum(xn * gx, axis=-1, keepdims=True)) * x_inv
    other = xg_ref[...]
    lanes = along_lanes(row_inverse(other))
    _, slope = loss_and_slope(by_rows(y, other) * (y_inv * tau) * lanes + offset)
    gy = (gy_in[...] + product((slope * lanes).astype(BF16), other)) * tau
    yn = y.astype(F32) * y_inv
    ty_ref[...] = (gy - yn * jnp.sum(yn * gy, axis=-1, keepdims=True)) * y_inv


def call(kernel, outs, flops, scale, bias, *args):
    return pl.pallas_call(
        kernel,
        out_shape=[jax.ShapeDtypeStruct(shape, F32) for shape in outs],
        in_specs=[pl.BlockSpec(memory_space=pltpu.SMEM)] * 2
        + [pl.BlockSpec(memory_space=pltpu.VMEM)] * len(args),
        out_specs=[pl.BlockSpec(memory_space=pltpu.VMEM)] * len(outs),
        compiler_params=pltpu.CompilerParams(vmem_limit_bytes=40 * 1024 * 1024),
        cost_estimate=pl.CostEstimate(flops=flops, bytes_accessed=8 * 1024 * 1024, transcendentals=0),
    )(scale, bias, *args)


def local(image_feats, text_feats, positive, scale, bias):
    x, y = image_feats, text_feats
    rows, width = x.shape
    index = lax.axis_index("blk")
    place = index % SPAN
    chip, core = place // CORES, place % CORES
    last = lax.axis_size("blk") - SPAN
    wrapped = around(jnp.where(index >= last, y, x))
    y_back = next_row(y, 1)
    x_next = next_row(x, -1)
    y_outer = shifted(y, "group", 1)
    x_outer = shifted(x, "group", -1)
    block = (rows, width)
    work = 2 * rows * rows * width

    def inner(_):
        up = jnp.concatenate([y, jnp.where(index >= last, wrapped, x_next)], axis=0)
        down = jnp.concatenate([jnp.where(index < SPAN, wrapped, y_back), x], axis=0)
        sends = [jnp.where(chip + by < CHIPS, up, down) for by in range(1, CHIPS)]
        twins = [to_twin(jnp.where(core == 0, up, down))]
        sends[1], twins[0] = lax.optimization_barrier((sends[1], twins[0]))
        pairs = [in_row(sends[by - 1], by) for by in range(1, CHIPS)]
        twins += [to_twin(pair) for pair in pairs]
        loss, gx, gy = call(
            inner_kernel, [(rows, rows), block, block], work * 31, scale, bias, x, y,
            positive, *pairs, *twins,
        )
        return loss, gx, gy

    def skip(_):
        return jnp.zeros((rows, rows), F32), jnp.zeros(block, F32), jnp.zeros(block, F32)

    go = lax.optimization_barrier(jnp.int32(1))
    loss, gx, gy = lax.cond(go > 0, inner, skip, 0)
    loss, image_grad, text_grad = call(
        outer_kernel, [(1, rows), block, block], work * 4, scale, bias, x, y, y_outer, x_outer, loss, gx, gy
    )
    return (loss[0], image_grad, text_grad)


def solution(mesh):
    rows = P(("blk", "group"), None)
    return jax.shard_map(
        local,
        mesh=mesh,
        in_specs=(rows, rows, rows, P(), P()),
        out_specs=(P(("blk", "group")), rows, rows),
        check_vma=False,
    )
```

```python
import functools

import jax
import jax.numpy as jnp
from jax import lax
from jax.experimental import pallas as pl
from jax.experimental.pallas import tpu as pltpu
from jax.sharding import PartitionSpec as P

SPAN = 8
CORES = 2
CHIPS = SPAN // CORES
F32 = jnp.float32
BF16 = jnp.bfloat16


def along_ring(x, by):
    blks, groups = lax.axis_size("blk"), lax.axis_size("group")
    length = blks // SPAN
    pairs = []
    for blk in range(blks):
        row, place = divmod(blk, SPAN)
        for group in range(groups):
            to = (group * length + row + by) % (groups * length)
            to_blk, to_group = to % length * SPAN + place, to // length
            pairs.append((blk * groups + group, to_blk * groups + to_group))
    return lax.ppermute(x, ("blk", "group"), pairs)


def in_row(x, by):
    pairs = []
    for i in range(lax.axis_size("blk")):
        first, place = i - i % SPAN, i % SPAN
        pairs.append((i, first + (place + CORES * by) % SPAN))
    return lax.ppermute(x, "blk", pairs)


def around(x):
    last = lax.axis_size("blk") - SPAN
    pairs = [(last + i, i) for i in range(SPAN)] + [(i, last + i) for i in range(SPAN)]
    return lax.ppermute(x, "blk", pairs)


def to_twin(x):
    return lax.ppermute(x, "blk", [(i, i ^ 1) for i in range(lax.axis_size("blk"))])


def row_inverse(values):
    floats = values.astype(F32)
    return lax.rsqrt(jnp.sum(floats * floats, axis=-1, keepdims=True) + 1e-06)


def along_lanes(column):
    rows = column.shape[0]
    return jnp.broadcast_to(column, (rows, rows)).T


def by_rows(left, right):
    return lax.dot_general(left, right, (((1,), (1,)), ((), ())), preferred_element_type=F32)


def by_cols(left, right):
    return lax.dot_general(left, right, (((0,), (0,)), ((), ())), preferred_element_type=F32)


def product(left, right):
    return jnp.dot(left, right, preferred_element_type=F32)


def loss_and_slope(u):
    small = jnp.exp(-jnp.abs(u))
    whole = 1.0 + small
    return (
        jnp.maximum(u, 0.0) + jnp.log1p(small),
        jnp.where(u >= 0.0, 1.0, small) / whole,
    )


def inner_kernel(scale, bias, x_ref, y_ref, pos_ref, *rest):
    pairs, (loss_ref, gx_ref, gy_ref) = rest[:-3], rest[-3:]
    tau, offset = scale[0], bias[0]
    rows = x_ref.shape[0]
    x, y = x_ref[...], y_ref[...]
    x_inv, y_inv = row_inverse(x), row_inverse(y)
    x_tau, y_tau = x_inv * tau, y_inv * tau
    y_lanes = along_lanes(y_inv)
    own = by_rows(x, y) * x_tau * y_lanes + offset
    place = lax.broadcasted_iota(jnp.int32, (rows, rows), 1).astype(F32)
    match = jnp.broadcast_to(pos_ref[...].astype(F32), (rows, rows)).T
    away = jnp.where(match == place, -1.0, 1.0)
    loss, slope = loss_and_slope(away * own)
    slope = slope * away
    gx = product((slope * y_lanes).astype(BF16), y)
    gy = by_cols((slope * x_inv).astype(BF16), x)
    for ref in pairs:
        other = ref[:rows, :]
        lanes = along_lanes(row_inverse(other))
        add, slope = loss_and_slope(by_rows(x, other) * x_tau * lanes + offset)
        loss = loss + add
        gx = gx + product((slope * lanes).astype(BF16), other)
        other = ref[rows:, :]
        lanes = along_lanes(row_inverse(other))
        _, slope = loss_and_slope(by_rows(y, other) * y_tau * lanes + offset)
        gy = gy + product((slope * lanes).astype(BF16), other)
    loss_ref[...] = loss
    gx_ref[...] = gx
    gy_ref[...] = gy


def outer_kernel(scale, bias, x_ref, y_ref, yg_ref, xg_ref, loss_in, gx_in, gy_in, loss_ref, ix_ref, ty_ref):
    tau, offset = scale[0], bias[0]
    rows = x_ref.shape[0]
    x, y = x_ref[...], y_ref[...]
    x_inv, y_inv = row_inverse(x), row_inverse(y)
    other = yg_ref[...]
    lanes = along_lanes(row_inverse(other))
    add, slope = loss_and_slope(by_rows(x, other) * (x_inv * tau) * lanes + offset)
    loss_ref[...] = jnp.sum((loss_in[...] + add).T, axis=0, keepdims=True) / F32((SPAN + 1) * rows)
    gx = (gx_in[...] + product((slope * lanes).astype(BF16), other)) * tau
    xn = x.astype(F32) * x_inv
    ix_ref[...] = (gx - xn * jnp.sum(xn * gx, axis=-1, keepdims=True)) * x_inv
    other = xg_ref[...]
    lanes = along_lanes(row_inverse(other))
    _, slope = loss_and_slope(by_rows(y, other) * (y_inv * tau) * lanes + offset)
    gy = (gy_in[...] + product((slope * lanes).astype(BF16), other)) * tau
    yn = y.astype(F32) * y_inv
    ty_ref[...] = (gy - yn * jnp.sum(yn * gy, axis=-1, keepdims=True)) * y_inv


def call(kernel, outs, flops, scale, bias, *args):
    return pl.pallas_call(
        kernel,
        out_shape=[jax.ShapeDtypeStruct(shape, F32) for shape in outs],
        in_specs=[pl.BlockSpec(memory_space=pltpu.SMEM)] * 2
        + [pl.BlockSpec(memory_space=pltpu.VMEM)] * len(args),
        out_specs=[pl.BlockSpec(memory_space=pltpu.VMEM)] * len(outs),
        compiler_params=pltpu.CompilerParams(vmem_limit_bytes=40 * 1024 * 1024),
        cost_estimate=pl.CostEstimate(flops=flops, bytes_accessed=8 * 1024 * 1024, transcendentals=0),
    )(scale, bias, *args)


def local(image_feats, text_feats, positive, scale, bias):
    x, y = image_feats, text_feats
    rows, width = x.shape
    index = lax.axis_index("blk")
    place = index % SPAN
    chip, core = place // CORES, place % CORES
    last = lax.axis_size("blk") - SPAN
    wrapped = around(jnp.where(index >= last, y, x))
    length = lax.axis_size("blk") // SPAN
    y_back = along_ring(y, 1)
    x_next = along_ring(x, -1)
    y_back, x_next, wrapped = lax.optimization_barrier((y_back, x_next, wrapped))
    y_outer = along_ring(y_back, length - 1)
    x_outer = along_ring(x_next, 1 - length)
    block = (rows, width)
    work = 2 * rows * rows * width

    def inner(_):
        up = jnp.concatenate([y, jnp.where(index >= last, wrapped, x_next)], axis=0)
        down = jnp.concatenate([jnp.where(index < SPAN, wrapped, y_back), x], axis=0)
        sends = [jnp.where(chip + by < CHIPS, up, down) for by in range(1, CHIPS)]
        twins = [to_twin(jnp.where(core == 0, up, down))]
        sends[1], twins[0] = lax.optimization_barrier((sends[1], twins[0]))
        pairs = [in_row(sends[by - 1], by) for by in range(1, CHIPS)]
        twins += [to_twin(pair) for pair in pairs]
        loss, gx, gy = call(
            inner_kernel, [(rows, rows), block, block], work * 31, scale, bias, x, y,
            positive, *pairs, *twins,
        )
        return loss, gx, gy

    def skip(_):
        return jnp.zeros((rows, rows), F32), jnp.zeros(block, F32), jnp.zeros(block, F32)

    go = lax.optimization_barrier(jnp.int32(1))
    loss, gx, gy = lax.cond(go > 0, inner, skip, 0)
    loss, image_grad, text_grad = call(
        outer_kernel, [(1, rows), block, block], work * 4, scale, bias, x, y, y_outer, x_outer, loss, gx, gy
    )
    return (loss[0], image_grad, text_grad)


def solution(mesh):
    rows = P(("blk", "group"), None)
    return jax.shard_map(
        local,
        mesh=mesh,
        in_specs=(rows, rows, rows, P(), P()),
        out_specs=(P(("blk", "group")), rows, rows),
        check_vma=False,
    )
```

```python
import functools

import jax
import jax.numpy as jnp
from jax import lax
from jax.experimental import pallas as pl
from jax.experimental.pallas import tpu as pltpu
from jax.sharding import PartitionSpec as P

SPAN = 8
CORES = 2
CHIPS = SPAN // CORES
F32 = jnp.float32
BF16 = jnp.bfloat16


def along_ring(x, by):
    blks, groups = lax.axis_size("blk"), lax.axis_size("group")
    length = blks // SPAN
    pairs = []
    for blk in range(blks):
        row, place = divmod(blk, SPAN)
        for group in range(groups):
            to = (group * length + row + by) % (groups * length)
            to_blk, to_group = to % length * SPAN + place, to // length
            pairs.append((blk * groups + group, to_blk * groups + to_group))
    return lax.ppermute(x, ("blk", "group"), pairs)


def in_row(x, by):
    pairs = []
    for i in range(lax.axis_size("blk")):
        first, place = i - i % SPAN, i % SPAN
        pairs.append((i, first + (place + CORES * by) % SPAN))
    return lax.ppermute(x, "blk", pairs)


def around(x):
    last = lax.axis_size("blk") - SPAN
    pairs = [(last + i, i) for i in range(SPAN)] + [(i, last + i) for i in range(SPAN)]
    return lax.ppermute(x, "blk", pairs)


def to_twin(x):
    return lax.ppermute(x, "blk", [(i, i ^ 1) for i in range(lax.axis_size("blk"))])


def row_inverse(values):
    floats = values.astype(F32)
    return lax.rsqrt(jnp.sum(floats * floats, axis=-1, keepdims=True) + 1e-06)


def unit_rows(values):
    return (values.astype(F32) * row_inverse(values)).astype(BF16)


def by_rows(left, right):
    return lax.dot_general(left, right, (((1,), (1,)), ((), ())), preferred_element_type=F32)


def by_cols(left, right):
    return lax.dot_general(left, right, (((0,), (0,)), ((), ())), preferred_element_type=F32)


def product(left, right):
    return jnp.dot(left, right, preferred_element_type=F32)


def loss_and_slope(u):
    small = jnp.exp(-jnp.abs(u))
    whole = 1.0 + small
    return (
        jnp.maximum(u, 0.0) + jnp.log1p(small),
        jnp.where(u >= 0.0, 1.0, small) / whole,
    )


TEXT, IMAGE = 0, 1


def add_block(other, role, tau, offset, units_ref, loss_ref, grads_ref):
    unit = unit_rows(other)
    loss, slope = loss_and_slope(tau * by_rows(units_ref[role], unit) + offset)
    loss_ref[...] += jnp.where(role == TEXT, loss, 0.0)
    grads_ref[role] += product(slope.astype(BF16), unit)


def add_blocks(roles, refs, tau, offset, units_ref, loss_ref, grads_ref):
    rows = units_ref.shape[1]
    singles, twin = refs[:-1], refs[-1]
    for by, ref in enumerate(singles, 1):
        add_block(ref[...], roles[by], tau, offset, units_ref, loss_ref, grads_ref)
    for by in range(CHIPS):
        add_block(twin[by * rows : (by + 1) * rows, :], roles[by], tau, offset, units_ref, loss_ref, grads_ref)


def first_kernel(scale, bias, roles, x_ref, y_ref, pos_ref, *rest):
    refs, (loss_ref, grads_ref, units_ref) = rest[:-3], rest[-3:]
    tau, offset = scale[0], bias[0]
    rows = x_ref.shape[0]
    x, y = unit_rows(x_ref[...]), unit_rows(y_ref[...])
    units_ref[IMAGE] = y
    units_ref[TEXT] = x
    logit = tau * by_rows(x, y) + offset
    place = lax.broadcasted_iota(jnp.int32, (rows, rows), 1).astype(F32)
    match = jnp.broadcast_to(pos_ref[...].astype(F32), (rows, rows)).T
    away = jnp.where(match == place, -1.0, 1.0)
    loss, slope = loss_and_slope(away * logit)
    slope = (slope * away).astype(BF16)
    loss_ref[...] = loss
    grads_ref[TEXT] = product(slope, y)
    grads_ref[IMAGE] = by_cols(slope, x)
    add_blocks(roles, refs, tau, offset, units_ref, loss_ref, grads_ref)


def second_kernel(scale, bias, roles, units_ref, loss_in, grads_in, *rest):
    refs, (loss_ref, grads_ref) = rest[:-2], rest[-2:]
    loss_ref[...] = loss_in[...]
    grads_ref[...] = grads_in[...]
    add_blocks(roles, refs, scale[0], bias[0], units_ref, loss_ref, grads_ref)


def last_kernel(scale, bias, x_ref, y_ref, yg_ref, xg_ref, units_ref, loss_in, grads_in, loss_ref, ix_ref, ty_ref):
    tau, offset = scale[0], bias[0]
    rows = x_ref.shape[0]
    unit = unit_rows(yg_ref[...])
    add, slope = loss_and_slope(tau * by_rows(units_ref[TEXT], unit) + offset)
    loss_ref[...] = jnp.sum((loss_in[...] + add).T, axis=0, keepdims=True) / F32((SPAN + 1) * rows)
    gx = (grads_in[TEXT] + product(slope.astype(BF16), unit)) * tau
    x = x_ref[...]
    x_inv = row_inverse(x)
    xn = x.astype(F32) * x_inv
    ix_ref[...] = (gx - xn * jnp.sum(xn * gx, axis=-1, keepdims=True)) * x_inv
    unit = unit_rows(xg_ref[...])
    _, slope = loss_and_slope(tau * by_rows(units_ref[IMAGE], unit) + offset)
    gy = (grads_in[IMAGE] + product(slope.astype(BF16), unit)) * tau
    y = y_ref[...]
    y_inv = row_inverse(y)
    yn = y.astype(F32) * y_inv
    ty_ref[...] = (gy - yn * jnp.sum(yn * gy, axis=-1, keepdims=True)) * y_inv


def call(kernel, outs, blocks, scalars, *args):
    flops = blocks * 4 * 128 * 128 * 1152
    return pl.pallas_call(
        kernel,
        out_shape=[jax.ShapeDtypeStruct(shape, kind) for shape, kind in outs],
        in_specs=[pl.BlockSpec(memory_space=pltpu.SMEM)] * len(scalars)
        + [pl.BlockSpec(memory_space=pltpu.VMEM)] * len(args),
        out_specs=[pl.BlockSpec(memory_space=pltpu.VMEM)] * len(outs),
        compiler_params=pltpu.CompilerParams(vmem_limit_bytes=40 * 1024 * 1024),
        cost_estimate=pl.CostEstimate(flops=flops, bytes_accessed=blocks * 1024 * 1024, transcendentals=0),
    )(*scalars, *args)


def local(image_feats, text_feats, positive, scale, bias):
    x, y = image_feats, text_feats
    rows, width = x.shape
    index = lax.axis_index("blk")
    place = index % SPAN
    chip, core = place // CORES, place % CORES
    last = lax.axis_size("blk") - SPAN
    length = lax.axis_size("blk") // SPAN
    shifts = range(1, CHIPS)
    wrapped = around(jnp.where(index >= last, y, x))
    y_back = along_ring(y, 1)
    x_next = along_ring(x, -1)
    first = {by: jnp.where(chip + by < CHIPS, y, x) for by in shifts}
    got = {by: in_row(first[by], by) for by in (1, CHIPS - 1)}
    first[2], got[1] = lax.optimization_barrier((first[2], got[1]))
    got[2] = in_row(first[2], 2)
    got = [got[by] for by in shifts]
    y_back, x_next, wrapped = lax.optimization_barrier((y_back, x_next, wrapped))
    y_outer = along_ring(y_back, length - 1)
    x_outer = along_ring(x_next, 1 - length)
    loss_out, grads_out = ((rows, rows), F32), ((2, rows, width), F32)
    units_out = ((2, rows, width), BF16)
    roles = jnp.stack([1 - core] + [(chip < by).astype(jnp.int32) for by in shifts])

    def inner(_):
        twin = to_twin(jnp.concatenate([jnp.where(core == 0, y, x)] + got, axis=0))
        loss, grads, units = call(
            first_kernel, [loss_out, grads_out, units_out], 8, (scale, bias, roles), x, y, positive, *got, twin
        )
        text = jnp.where(index < SPAN, wrapped, y_back)
        image = jnp.where(index >= last, wrapped, x_next)
        then = [jnp.where(chip + by < CHIPS, image, text) for by in shifts]
        then[1], twin = lax.optimization_barrier((then[1], twin))
        later = [in_row(block, by) for by, block in zip(shifts, then)]
        twin = to_twin(jnp.concatenate([jnp.where(core == 0, image, text)] + later, axis=0))
        loss, grads = call(
            second_kernel, [loss_out, grads_out], 7, (scale, bias, 1 - roles), units, loss, grads, *later, twin
        )
        return loss, grads, units

    def skip(_):
        return tuple(jnp.zeros(*out) for out in (loss_out, grads_out, units_out))

    go = lax.optimization_barrier(jnp.int32(1))
    loss, grads, units = lax.cond(go > 0, inner, skip, 0)
    block = ((rows, width), F32)
    loss, image_grad, text_grad = call(
        last_kernel, [((1, rows), F32), block, block], 2, (scale, bias), x, y, y_outer, x_outer, units, loss, grads
    )
    return (loss[0], image_grad, text_grad)


def solution(mesh):
    rows = P(("blk", "group"), None)
    return jax.shard_map(
        local,
        mesh=mesh,
        in_specs=(rows, rows, rows, P(), P()),
        out_specs=(P(("blk", "group")), rows, rows),
        check_vma=False,
    )
```

```python
import functools

import jax
import jax.numpy as jnp
from jax import lax
from jax.experimental import pallas as pl
from jax.experimental.pallas import tpu as pltpu
from jax.sharding import PartitionSpec as P

SPAN = 8
CORES = 2
CHIPS = SPAN // CORES
F32 = jnp.float32
BF16 = jnp.bfloat16


def along_ring(x, by):
    blks, groups = lax.axis_size("blk"), lax.axis_size("group")
    length = blks // SPAN
    pairs = []
    for blk in range(blks):
        row, place = divmod(blk, SPAN)
        for group in range(groups):
            to = (group * length + row + by) % (groups * length)
            to_blk, to_group = to % length * SPAN + place, to // length
            pairs.append((blk * groups + group, to_blk * groups + to_group))
    return lax.ppermute(x, ("blk", "group"), pairs)


def in_row(x, by):
    pairs = []
    for i in range(lax.axis_size("blk")):
        first, place = i - i % SPAN, i % SPAN
        pairs.append((i, first + (place + CORES * by) % SPAN))
    return lax.ppermute(x, "blk", pairs)


def around(x):
    last = lax.axis_size("blk") - SPAN
    pairs = [(last + i, i) for i in range(SPAN)] + [(i, last + i) for i in range(SPAN)]
    return lax.ppermute(x, "blk", pairs)


def to_twin(x):
    return lax.ppermute(x, "blk", [(i, i ^ 1) for i in range(lax.axis_size("blk"))])


def row_inverse(values):
    floats = values.astype(F32)
    return lax.rsqrt(jnp.sum(floats * floats, axis=-1, keepdims=True) + 1e-06)


def unit_rows(values):
    return (values.astype(F32) * row_inverse(values)).astype(BF16)


def by_rows(left, right):
    return lax.dot_general(left, right, (((1,), (1,)), ((), ())), preferred_element_type=F32)


def by_cols(left, right):
    return lax.dot_general(left, right, (((0,), (0,)), ((), ())), preferred_element_type=F32)


def product(left, right):
    return jnp.dot(left, right, preferred_element_type=F32)


def loss_and_slope(u):
    small = jnp.exp(-jnp.abs(u))
    whole = 1.0 + small
    return (
        jnp.maximum(u, 0.0) + jnp.log1p(small),
        jnp.where(u >= 0.0, 1.0, small) / whole,
    )


TEXT, IMAGE = 0, 1


def add_block(other, role, tau, offset, units_ref, loss_ref, grads_ref):
    unit = unit_rows(other)
    loss, slope = loss_and_slope(tau * by_rows(units_ref[role], unit) + offset)
    loss_ref[...] += jnp.where(role == TEXT, loss, 0.0)
    grads_ref[role] += product(slope.astype(BF16), unit)


def add_blocks(roles, refs, tau, offset, units_ref, loss_ref, grads_ref):
    rows = units_ref.shape[1]
    at = 0
    for ref in refs:
        for first in range(0, ref.shape[0], rows):
            add_block(ref[first : first + rows, :], roles[at], tau, offset, units_ref, loss_ref, grads_ref)
            at += 1


def first_kernel(scale, bias, roles, x_ref, y_ref, pos_ref, *rest):
    refs, (loss_ref, grads_ref, units_ref) = rest[:-3], rest[-3:]
    tau, offset = scale[0], bias[0]
    rows = x_ref.shape[0]
    x, y = unit_rows(x_ref[...]), unit_rows(y_ref[...])
    units_ref[IMAGE] = y
    units_ref[TEXT] = x
    logit = tau * by_rows(x, y) + offset
    place = lax.broadcasted_iota(jnp.int32, (rows, rows), 1).astype(F32)
    match = jnp.broadcast_to(pos_ref[...].astype(F32), (rows, rows)).T
    away = jnp.where(match == place, -1.0, 1.0)
    loss, slope = loss_and_slope(away * logit)
    slope = (slope * away).astype(BF16)
    loss_ref[...] = loss
    grads_ref[TEXT] = product(slope, y)
    grads_ref[IMAGE] = by_cols(slope, x)
    add_blocks(roles, refs, tau, offset, units_ref, loss_ref, grads_ref)


def next_kernel(scale, bias, roles, units_ref, loss_in, grads_in, *rest):
    refs, (loss_ref, grads_ref) = rest[:-2], rest[-2:]
    loss_ref[...] = loss_in[...]
    grads_ref[...] = grads_in[...]
    add_blocks(roles, refs, scale[0], bias[0], units_ref, loss_ref, grads_ref)


def outer_grad(tau, offset, feats_ref, other_ref, unit, before):
    other = unit_rows(other_ref[...])
    loss, slope = loss_and_slope(tau * by_rows(unit, other) + offset)
    grad = (before + product(slope.astype(BF16), other)) * tau
    feats = feats_ref[...]
    inverse = row_inverse(feats)
    norm = feats.astype(F32) * inverse
    return loss, (grad - norm * jnp.sum(norm * grad, axis=-1, keepdims=True)) * inverse


def image_kernel(scale, bias, x_ref, other_ref, units_ref, loss_in, grads_in, loss_ref, out_ref):
    loss, out_ref[...] = outer_grad(scale[0], bias[0], x_ref, other_ref, units_ref[TEXT], grads_in[TEXT])
    rows = x_ref.shape[0]
    loss_ref[...] = jnp.sum((loss_in[...] + loss).T, axis=0, keepdims=True) / F32((SPAN + 1) * rows)


def text_kernel(scale, bias, y_ref, other_ref, units_ref, grads_in, out_ref):
    _, out_ref[...] = outer_grad(scale[0], bias[0], y_ref, other_ref, units_ref[IMAGE], grads_in[IMAGE])


def call(kernel, outs, blocks, scalars, *args):
    flops = blocks * 4 * 128 * 128 * 1152
    return pl.pallas_call(
        kernel,
        out_shape=[jax.ShapeDtypeStruct(shape, kind) for shape, kind in outs],
        in_specs=[pl.BlockSpec(memory_space=pltpu.SMEM)] * len(scalars)
        + [pl.BlockSpec(memory_space=pltpu.VMEM)] * len(args),
        out_specs=[pl.BlockSpec(memory_space=pltpu.VMEM)] * len(outs),
        compiler_params=pltpu.CompilerParams(vmem_limit_bytes=40 * 1024 * 1024),
        cost_estimate=pl.CostEstimate(flops=flops, bytes_accessed=blocks * 1024 * 1024, transcendentals=0),
    )(*scalars, *args)


def local(image_feats, text_feats, positive, scale, bias):
    x, y = image_feats, text_feats
    rows, width = x.shape
    index = lax.axis_index("blk")
    place = index % SPAN
    chip, core = place // CORES, place % CORES
    last = lax.axis_size("blk") - SPAN
    length = lax.axis_size("blk") // SPAN
    shifts = range(1, CHIPS)
    wrapped = around(jnp.where(index >= last, y, x))
    y_back = along_ring(y, 1)
    x_next = along_ring(x, -1)
    first = {by: jnp.where(chip + by < CHIPS, y, x) for by in shifts}
    got = {by: in_row(first[by], by) for by in (1, CHIPS - 1)}
    first[2], got[1] = lax.optimization_barrier((first[2], got[1]))
    got[2] = in_row(first[2], 2)
    got = [got[by] for by in shifts]
    y_outer = along_ring(y_back, length - 1)
    x_outer = along_ring(x_next, 1 - length)
    loss_out, grads_out = ((rows, rows), F32), ((2, rows, width), F32)
    units_out = ((2, rows, width), BF16)
    from_chips = [(chip < by).astype(jnp.int32) for by in shifts]
    roles = jnp.stack(from_chips + [1 - core] + from_chips)

    def inner(_):
        twin = to_twin(jnp.concatenate([jnp.where(core == 0, y, x)] + got, axis=0))
        loss, grads, units = call(
            first_kernel, [loss_out, grads_out, units_out], 8, (scale, bias, roles), x, y, positive, *got, twin
        )
        text = jnp.where(index < SPAN, wrapped, y_back)
        image = jnp.where(index >= last, wrapped, x_next)
        then = [jnp.where(chip + by < CHIPS, image, text) for by in shifts]
        then[1], twin = lax.optimization_barrier((then[1], twin))
        later = [in_row(block, by) for by, block in zip(shifts, then)]
        *later, loss = lax.optimization_barrier((*later, loss))
        twin = to_twin(jnp.concatenate([jnp.where(core == 0, image, text)] + later, axis=0))
        outs, count = [loss_out, grads_out], len(later)
        loss, grads = call(
            next_kernel, outs, count, (scale, bias, 1 - roles[:count]), units, loss, grads, *later
        )
        loss, grads = call(
            next_kernel, outs, count + 1, (scale, bias, 1 - roles[count:]), units, loss, grads, twin
        )
        return loss, grads, units

    def skip(_):
        return tuple(jnp.zeros(*out) for out in (loss_out, grads_out, units_out))

    go = lax.optimization_barrier(jnp.int32(1))
    loss, grads, units = lax.cond(go > 0, inner, skip, 0)
    block = ((rows, width), F32)
    loss, image_grad = call(
        image_kernel, [((1, rows), F32), block], 1, (scale, bias), x, y_outer, units, loss, grads
    )
    (text_grad,) = call(text_kernel, [block], 1, (scale, bias), y, x_outer, units, grads)
    return (loss[0], image_grad, text_grad)


def solution(mesh):
    rows = P(("blk", "group"), None)
    return jax.shard_map(
        local,
        mesh=mesh,
        in_specs=(rows, rows, rows, P(), P()),
        out_specs=(P(("blk", "group")), rows, rows),
        check_vma=False,
    )
```

```python
import functools

import jax
import jax.numpy as jnp
from jax import lax
from jax.experimental import pallas as pl
from jax.experimental.pallas import tpu as pltpu
from jax.sharding import PartitionSpec as P

SPAN = 8
CORES = 2
CHIPS = SPAN // CORES
F32 = jnp.float32
BF16 = jnp.bfloat16


def along_ring(x, by):
    blks, groups = lax.axis_size("blk"), lax.axis_size("group")
    length = blks // SPAN
    pairs = []
    for blk in range(blks):
        row, place = divmod(blk, SPAN)
        for group in range(groups):
            to = (group * length + row + by) % (groups * length)
            to_blk, to_group = to % length * SPAN + place, to // length
            pairs.append((blk * groups + group, to_blk * groups + to_group))
    return lax.ppermute(x, ("blk", "group"), pairs)


def in_row(x, by):
    pairs = []
    for i in range(lax.axis_size("blk")):
        first, place = i - i % SPAN, i % SPAN
        pairs.append((i, first + (place + CORES * by) % SPAN))
    return lax.ppermute(x, "blk", pairs)


def around(x):
    last = lax.axis_size("blk") - SPAN
    pairs = [(last + i, i) for i in range(SPAN)] + [(i, last + i) for i in range(SPAN)]
    return lax.ppermute(x, "blk", pairs)


def to_twin(x):
    return lax.ppermute(x, "blk", [(i, i ^ 1) for i in range(lax.axis_size("blk"))])


def row_inverse(values):
    floats = values.astype(F32)
    return lax.rsqrt(jnp.sum(floats * floats, axis=-1, keepdims=True) + 1e-06)


def unit_rows(values):
    return (values.astype(F32) * row_inverse(values)).astype(BF16)


def by_rows(left, right):
    return lax.dot_general(left, right, (((1,), (1,)), ((), ())), preferred_element_type=F32)


def by_cols(left, right):
    return lax.dot_general(left, right, (((0,), (0,)), ((), ())), preferred_element_type=F32)


def product(left, right):
    return jnp.dot(left, right, preferred_element_type=F32)


def loss_and_slope(u):
    small = jnp.exp(-jnp.abs(u))
    whole = 1.0 + small
    return (
        jnp.maximum(u, 0.0) + jnp.log1p(small),
        jnp.where(u >= 0.0, 1.0, small) / whole,
    )


TEXT, IMAGE = 0, 1


def add_blocks(roles, refs, tau, offset, units, loss_ref, grads_ref, stack_ref):
    rows = units.shape[0] // 2
    at = 0
    for ref in refs:
        for first in range(0, ref.shape[0], rows):
            stack_ref[at : at + rows, :] = unit_rows(ref[first : first + rows, :])
            at += rows
    stack = stack_ref[...]
    logits = tau * by_rows(stack, units) + offset
    slopes = []
    for i in range(at // rows):
        is_text = roles[i] == TEXT
        block = logits[i * rows : (i + 1) * rows, :]
        loss, slope = loss_and_slope(jnp.where(is_text, block[:, :rows], block[:, rows:]))
        loss_ref[...] += jnp.where(is_text, loss, 0.0)
        text, image = jnp.where(is_text, slope, 0.0), jnp.where(is_text, 0.0, slope)
        slopes.append(jnp.concatenate([text, image], axis=1).astype(BF16))
    grads_ref[...] += by_cols(jnp.concatenate(slopes, axis=0), stack)


def first_kernel(scale, bias, roles, x_ref, y_ref, pos_ref, *rest):
    refs, (loss_ref, grads_ref, units_ref, inverses_ref, stack_ref) = rest[:-5], rest[-5:]
    tau, offset = scale[0], bias[0]
    rows = x_ref.shape[0]
    for i, ref in enumerate((x_ref, y_ref)):
        inverse = row_inverse(ref[...])
        inverses_ref[i * rows : (i + 1) * rows, :] = inverse
        units_ref[i * rows : (i + 1) * rows, :] = (ref[...].astype(F32) * inverse).astype(BF16)
    units = units_ref[...]
    x, y = units[:rows, :], units[rows:, :]
    place = lax.broadcasted_iota(jnp.int32, (rows, rows), 0)
    away = jnp.where(place == pos_ref[...], -1.0, 1.0)
    loss, slope = loss_and_slope(away * (tau * by_rows(y, x) + offset))
    slope = (slope * away).astype(BF16)
    loss_ref[...] = loss
    grads_ref[:rows, :] = by_cols(slope, y)
    grads_ref[rows:, :] = product(slope, x)
    add_blocks(roles, refs, tau, offset, units, loss_ref, grads_ref, stack_ref)


def next_kernel(scale, bias, roles, units_ref, loss_in, grads_in, *rest):
    refs, (loss_ref, grads_ref, stack_ref) = rest[:-3], rest[-3:]
    loss_ref[...] = loss_in[...]
    grads_ref[...] = grads_in[...]
    add_blocks(roles, refs, scale[0], bias[0], units_ref[...], loss_ref, grads_ref, stack_ref)


def last_kernel(
    scale, bias, x_ref, y_ref, yg_ref, xg_ref, units_ref, inverses_ref, loss_in, grads_in, loss_ref, ix_ref, ty_ref
):
    tau, offset = scale[0], bias[0]
    rows = x_ref.shape[0]
    for i, (feats_ref, other_ref, out_ref) in enumerate(((x_ref, yg_ref, ix_ref), (y_ref, xg_ref, ty_ref))):
        own = slice(i * rows, (i + 1) * rows)
        other = unit_rows(other_ref[...])
        loss, slope = loss_and_slope(tau * by_rows(other, units_ref[own, :]) + offset)
        if i == TEXT:
            loss_ref[...] = jnp.sum(loss_in[...] + loss, axis=0, keepdims=True) / F32((SPAN + 1) * rows)
        grad = (grads_in[own, :] + by_cols(slope.astype(BF16), other)) * tau
        inverse = inverses_ref[own, :]
        norm = feats_ref[...].astype(F32) * inverse
        out_ref[...] = (grad - norm * jnp.sum(norm * grad, axis=-1, keepdims=True)) * inverse


def call(kernel, outs, blocks, scalars, *args, scratch=()):
    flops = blocks * 4 * 128 * 128 * 1152
    return pl.pallas_call(
        kernel,
        out_shape=[jax.ShapeDtypeStruct(shape, kind) for shape, kind in outs],
        in_specs=[pl.BlockSpec(memory_space=pltpu.SMEM)] * len(scalars)
        + [pl.BlockSpec(memory_space=pltpu.VMEM)] * len(args),
        out_specs=[pl.BlockSpec(memory_space=pltpu.VMEM)] * len(outs),
        scratch_shapes=scratch,
        compiler_params=pltpu.CompilerParams(vmem_limit_bytes=40 * 1024 * 1024),
        cost_estimate=pl.CostEstimate(flops=flops, bytes_accessed=blocks * 1024 * 1024, transcendentals=0),
    )(*scalars, *args)


def local(image_feats, text_feats, positive, scale, bias):
    x, y = image_feats, text_feats
    rows, width = x.shape
    index = lax.axis_index("blk")
    place = index % SPAN
    chip, core = place // CORES, place % CORES
    last = lax.axis_size("blk") - SPAN
    length = lax.axis_size("blk") // SPAN
    shifts = range(1, CHIPS)
    wrapped = around(jnp.where(index >= last, y, x))
    y_back = along_ring(y, 1)
    x_next = along_ring(x, -1)
    first = [jnp.where(chip + by < CHIPS, y, x) for by in shifts]
    nearest = in_row(first[0], 1)
    y_outer = along_ring(y_back, length - 1)
    x_outer = along_ring(x_next, 1 - length)
    double = 2 * rows
    loss_out, grads_out = ((rows, rows), F32), ((double, width), F32)
    units_out, inverses_out = ((double, width), BF16), ((double, 1), F32)
    from_chips = [(chip < by).astype(jnp.int32) for by in shifts]
    roles = jnp.stack(from_chips + [1 - core] + from_chips)

    def stack(blocks):
        return [pltpu.VMEM((blocks * rows, width), BF16)]

    def inner(_):
        text = jnp.where(index < SPAN, wrapped, y_back)
        image = jnp.where(index >= last, wrapped, x_next)
        then = [jnp.where(chip + by < CHIPS, image, text) for by in shifts]
        got = [nearest, in_row(first[1], 2), in_row(first[2], 3)]
        then[2], got[2] = lax.optimization_barrier((then[2], got[2]))
        twin = to_twin(jnp.concatenate([jnp.where(core == 0, y, x)] + got, axis=0))
        then[1], twin = lax.optimization_barrier((then[1], twin))
        loss, grads, units, inverses = call(
            first_kernel, [loss_out, grads_out, units_out, inverses_out], 8, (scale, bias, roles),
            x, y, positive, *got, twin, scratch=stack(7),
        )
        later = [in_row(block, by) for by, block in zip(shifts, then)]
        *later, loss = lax.optimization_barrier((*later, loss))
        twin = to_twin(jnp.concatenate([jnp.where(core == 0, image, text)] + later, axis=0))
        outs, count = [loss_out, grads_out], len(later)
        loss, grads = call(
            next_kernel, outs, count, (scale, bias, 1 - roles[:count]),
            units, loss, grads, *later, scratch=stack(count),
        )
        loss, grads = call(
            next_kernel, outs, count + 1, (scale, bias, 1 - roles[count:]),
            units, loss, grads, twin, scratch=stack(count + 1),
        )
        return loss, grads, units, inverses

    def skip(_):
        return tuple(jnp.zeros(*out) for out in (loss_out, grads_out, units_out, inverses_out))

    go = lax.optimization_barrier(jnp.int32(1))
    loss, grads, units, inverses = lax.cond(go > 0, inner, skip, 0)
    block = ((rows, width), F32)
    loss, image_grad, text_grad = call(
        last_kernel, [((1, rows), F32), block, block], 2, (scale, bias),
        x, y, y_outer, x_outer, units, inverses, loss, grads,
    )
    return (loss[0], image_grad, text_grad)


def solution(mesh):
    rows = P(("blk", "group"), None)
    return jax.shard_map(
        local,
        mesh=mesh,
        in_specs=(rows, rows, rows, P(), P()),
        out_specs=(P(("blk", "group")), rows, rows),
        check_vma=False,
    )
```

```python
import functools

import jax
import jax.numpy as jnp
from jax import lax
from jax.experimental import pallas as pl
from jax.experimental.pallas import tpu as pltpu
from jax.sharding import PartitionSpec as P

SPAN = 8
CORES = 2
CHIPS = SPAN // CORES
F32 = jnp.float32
BF16 = jnp.bfloat16


def along_ring(x, by):
    blks, groups = lax.axis_size("blk"), lax.axis_size("group")
    length = blks // SPAN
    pairs = []
    for blk in range(blks):
        row, place = divmod(blk, SPAN)
        for group in range(groups):
            to = (group * length + row + by) % (groups * length)
            to_blk, to_group = to % length * SPAN + place, to // length
            pairs.append((blk * groups + group, to_blk * groups + to_group))
    return lax.ppermute(x, ("blk", "group"), pairs)


def in_row(x, by):
    pairs = []
    for i in range(lax.axis_size("blk")):
        first, place = i - i % SPAN, i % SPAN
        pairs.append((i, first + (place + CORES * by) % SPAN))
    return lax.ppermute(x, "blk", pairs)


def around(x):
    last = lax.axis_size("blk") - SPAN
    pairs = [(last + i, i) for i in range(SPAN)] + [(i, last + i) for i in range(SPAN)]
    return lax.ppermute(x, "blk", pairs)


def to_twin(x):
    return lax.ppermute(x, "blk", [(i, i ^ 1) for i in range(lax.axis_size("blk"))])


def row_inverse(values):
    floats = values.astype(F32)
    return lax.rsqrt(jnp.sum(floats * floats, axis=-1, keepdims=True) + 1e-06)


def unit_rows(values):
    return (values.astype(F32) * row_inverse(values)).astype(BF16)


def by_rows(left, right):
    return lax.dot_general(left, right, (((1,), (1,)), ((), ())), preferred_element_type=F32)


def by_cols(left, right):
    return lax.dot_general(left, right, (((0,), (0,)), ((), ())), preferred_element_type=F32)


def product(left, right):
    return jnp.dot(left, right, preferred_element_type=F32)


def loss_and_slope(u):
    small = jnp.exp(-jnp.abs(u))
    whole = 1.0 + small
    return (
        jnp.maximum(u, 0.0) + jnp.log1p(small),
        jnp.where(u >= 0.0, 1.0, small) / whole,
    )


TEXT, IMAGE = 0, 1


def add_blocks(roles, refs, tau, offset, units, loss_ref, grads_ref, stack_ref):
    rows = units.shape[0] // 2
    at = 0
    for ref in refs:
        for first in range(0, ref.shape[0], rows):
            stack_ref[at : at + rows, :] = unit_rows(ref[first : first + rows, :])
            at += rows
    stack = stack_ref[...]
    logits = tau * by_rows(stack, units) + offset
    slopes = []
    for i in range(at // rows):
        is_text = roles[i] == TEXT
        block = logits[i * rows : (i + 1) * rows, :]
        loss, slope = loss_and_slope(jnp.where(is_text, block[:, :rows], block[:, rows:]))
        loss_ref[...] += jnp.where(is_text, loss, 0.0)
        text, image = jnp.where(is_text, slope, 0.0), jnp.where(is_text, 0.0, slope)
        slopes.append(jnp.concatenate([text, image], axis=1).astype(BF16))
    grads_ref[...] += by_cols(jnp.concatenate(slopes, axis=0), stack)


def first_kernel(scale, bias, roles, x_ref, y_ref, pos_ref, *rest):
    refs, (loss_ref, grads_ref, units_ref, inverses_ref, stack_ref) = rest[:-5], rest[-5:]
    tau, offset = scale[0], bias[0]
    rows = x_ref.shape[0]
    for i, ref in enumerate((x_ref, y_ref)):
        inverse = row_inverse(ref[...])
        inverses_ref[i * rows : (i + 1) * rows, :] = inverse
        units_ref[i * rows : (i + 1) * rows, :] = (ref[...].astype(F32) * inverse).astype(BF16)
    units = units_ref[...]
    x, y = units[:rows, :], units[rows:, :]
    place = lax.broadcasted_iota(jnp.int32, (rows, rows), 0)
    away = jnp.where(place == pos_ref[...], -1.0, 1.0)
    loss, slope = loss_and_slope(away * (tau * by_rows(y, x) + offset))
    slope = (slope * away).astype(BF16)
    loss_ref[...] = loss
    grads_ref[:rows, :] = by_cols(slope, y)
    grads_ref[rows:, :] = product(slope, x)
    add_blocks(roles, refs, tau, offset, units, loss_ref, grads_ref, stack_ref)


def next_kernel(scale, bias, roles, units_ref, loss_in, grads_in, *rest):
    refs, (loss_ref, grads_ref, stack_ref) = rest[:-3], rest[-3:]
    loss_ref[...] = loss_in[...]
    grads_ref[...] = grads_in[...]
    add_blocks(roles, refs, scale[0], bias[0], units_ref[...], loss_ref, grads_ref, stack_ref)


def last_kernel(
    scale, bias, x_ref, y_ref, yg_ref, xg_ref, units_ref, inverses_ref, loss_in, grads_in, loss_ref, ix_ref, ty_ref
):
    tau, offset = scale[0], bias[0]
    rows = x_ref.shape[0]
    for i, (feats_ref, other_ref, out_ref) in enumerate(((x_ref, yg_ref, ix_ref), (y_ref, xg_ref, ty_ref))):
        own = slice(i * rows, (i + 1) * rows)
        other = unit_rows(other_ref[...])
        loss, slope = loss_and_slope(tau * by_rows(other, units_ref[own, :]) + offset)
        if i == TEXT:
            loss_ref[...] = jnp.sum(loss_in[...] + loss, axis=0, keepdims=True) / F32((SPAN + 1) * rows)
        grad = (grads_in[own, :] + by_cols(slope.astype(BF16), other)) * tau
        inverse = inverses_ref[own, :]
        norm = feats_ref[...].astype(F32) * inverse
        out_ref[...] = (grad - norm * jnp.sum(norm * grad, axis=-1, keepdims=True)) * inverse


def call(kernel, outs, blocks, scalars, *args, scratch=()):
    flops = blocks * 4 * 128 * 128 * 1152
    return pl.pallas_call(
        kernel,
        out_shape=[jax.ShapeDtypeStruct(shape, kind) for shape, kind in outs],
        in_specs=[pl.BlockSpec(memory_space=pltpu.SMEM)] * len(scalars)
        + [pl.BlockSpec(memory_space=pltpu.VMEM)] * len(args),
        out_specs=[pl.BlockSpec(memory_space=pltpu.VMEM)] * len(outs),
        scratch_shapes=scratch,
        compiler_params=pltpu.CompilerParams(vmem_limit_bytes=40 * 1024 * 1024),
        cost_estimate=pl.CostEstimate(flops=flops, bytes_accessed=blocks * 1024 * 1024, transcendentals=0),
    )(*scalars, *args)


def local(image_feats, text_feats, positive, scale, bias):
    x, y = image_feats, text_feats
    rows, width = x.shape
    index = lax.axis_index("blk")
    place = index % SPAN
    chip, core = place // CORES, place % CORES
    last = lax.axis_size("blk") - SPAN
    length = lax.axis_size("blk") // SPAN
    shifts = range(1, CHIPS)
    wrapped = around(jnp.where(index >= last, y, x))
    y_back = along_ring(y, 1)
    x_next = along_ring(x, -1)
    first = [jnp.where(chip + by < CHIPS, y, x) for by in shifts]
    near, far = in_row(first[0], 1), in_row(first[2], 3)
    y_outer, wrapped = lax.optimization_barrier((y_back, wrapped))
    x_outer, wrapped = lax.optimization_barrier((x_next, wrapped))
    y_outer = along_ring(y_outer, length - 1)
    x_outer = along_ring(x_outer, 1 - length)
    double = 2 * rows
    loss_out, grads_out = ((rows, rows), F32), ((double, width), F32)
    units_out, inverses_out = ((double, width), BF16), ((double, 1), F32)
    near_role, middle_role, far_role = [(chip < by).astype(jnp.int32) for by in shifts]
    twin_role = 1 - core

    def stack(blocks):
        return [pltpu.VMEM((blocks * rows, width), BF16)]

    def inner(_):
        text = jnp.where(index < SPAN, wrapped, y_back)
        image = jnp.where(index >= last, wrapped, x_next)
        then = [jnp.where(chip + by < CHIPS, image, text) for by in shifts]
        mine, other = jnp.where(core == 0, y, x), jnp.where(core == 0, image, text)
        twin = to_twin(jnp.concatenate([mine, near, far], axis=0))
        middle = in_row(first[1], 2)
        then[2], twin = lax.optimization_barrier((then[2], twin))
        then[1], middle = lax.optimization_barrier((then[1], middle))
        scalars = (scale, bias, jnp.stack([near_role, far_role, twin_role, near_role, far_role]))
        loss, grads, units, inverses = call(
            first_kernel, [loss_out, grads_out, units_out, inverses_out], 6, scalars,
            x, y, positive, near, far, twin, scratch=stack(5),
        )
        later = [in_row(block, by) for by, block in zip(shifts, then)] + [middle]
        *later, loss = lax.optimization_barrier((*later, loss))
        twin = to_twin(jnp.concatenate([other] + later, axis=0))
        later_roles = [1 - near_role, 1 - middle_role, 1 - far_role, middle_role]
        for roles, refs in ((later_roles, later), ([1 - twin_role] + later_roles, [twin])):
            loss, grads = call(
                next_kernel, [loss_out, grads_out], len(roles), (scale, bias, jnp.stack(roles)),
                units, loss, grads, *refs, scratch=stack(len(roles)),
            )
        return loss, grads, units, inverses

    def skip(_):
        return tuple(jnp.zeros(*out) for out in (loss_out, grads_out, units_out, inverses_out))

    go = lax.optimization_barrier(jnp.int32(1))
    loss, grads, units, inverses = lax.cond(go > 0, inner, skip, 0)
    block = ((rows, width), F32)
    loss, image_grad, text_grad = call(
        last_kernel, [((1, rows), F32), block, block], 2, (scale, bias),
        x, y, y_outer, x_outer, units, inverses, loss, grads,
    )
    return (loss[0], image_grad, text_grad)


def solution(mesh):
    rows = P(("blk", "group"), None)
    return jax.shard_map(
        local,
        mesh=mesh,
        in_specs=(rows, rows, rows, P(), P()),
        out_specs=(P(("blk", "group")), rows, rows),
        check_vma=False,
    )
```

```python
import functools

import jax
import jax.numpy as jnp
from jax import lax
from jax.experimental import pallas as pl
from jax.experimental.pallas import tpu as pltpu
from jax.sharding import PartitionSpec as P

SPAN = 8
CORES = 2
CHIPS = SPAN // CORES
F32 = jnp.float32
BF16 = jnp.bfloat16


def along_ring(x, by):
    blks, groups = lax.axis_size("blk"), lax.axis_size("group")
    length = blks // SPAN
    pairs = []
    for blk in range(blks):
        row, place = divmod(blk, SPAN)
        for group in range(groups):
            to = (group * length + row + by) % (groups * length)
            to_blk, to_group = to % length * SPAN + place, to // length
            pairs.append((blk * groups + group, to_blk * groups + to_group))
    return lax.ppermute(x, ("blk", "group"), pairs)


def swapped_along_ring(x, by, odd):
    blks, groups = lax.axis_size("blk"), lax.axis_size("group")
    length = blks // SPAN
    pairs = []
    for blk in range(blks):
        row, place = divmod(blk, SPAN)
        for group in range(groups):
            way = by if row % 2 == odd else -by
            to = (group * length + row + way) % (groups * length)
            to_blk, to_group = to % length * SPAN + place, to // length
            pairs.append((blk * groups + group, to_blk * groups + to_group))
    return lax.ppermute(x, ("blk", "group"), pairs)


def in_row(x, by):
    pairs = []
    for i in range(lax.axis_size("blk")):
        first, place = i - i % SPAN, i % SPAN
        pairs.append((i, first + (place + CORES * by) % SPAN))
    return lax.ppermute(x, "blk", pairs)


def around(x):
    last = lax.axis_size("blk") - SPAN
    pairs = [(last + i, i) for i in range(SPAN)] + [(i, last + i) for i in range(SPAN)]
    return lax.ppermute(x, "blk", pairs)


def to_twin(x):
    return lax.ppermute(x, "blk", [(i, i ^ 1) for i in range(lax.axis_size("blk"))])


def row_inverse(values):
    floats = values.astype(F32)
    return lax.rsqrt(jnp.sum(floats * floats, axis=-1, keepdims=True) + 1e-06)


def unit_rows(values):
    return (values.astype(F32) * row_inverse(values)).astype(BF16)


def by_rows(left, right):
    return lax.dot_general(left, right, (((1,), (1,)), ((), ())), preferred_element_type=F32)


def by_cols(left, right):
    return lax.dot_general(left, right, (((0,), (0,)), ((), ())), preferred_element_type=F32)


def product(left, right):
    return jnp.dot(left, right, preferred_element_type=F32)


def loss_and_slope(u):
    small = jnp.exp(-jnp.abs(u))
    whole = 1.0 + small
    return (
        jnp.maximum(u, 0.0) + jnp.log1p(small),
        jnp.where(u >= 0.0, 1.0, small) / whole,
    )


TEXT, IMAGE = 0, 1


def add_blocks(roles, refs, tau, offset, units, loss_ref, grads_ref, stack_ref):
    rows = units.shape[0] // 2
    at = 0
    for ref in refs:
        for first in range(0, ref.shape[0], rows):
            stack_ref[at : at + rows, :] = unit_rows(ref[first : first + rows, :])
            at += rows
    stack = stack_ref[...]
    logits = tau * by_rows(stack, units) + offset
    slopes = []
    for i in range(at // rows):
        is_text = roles[i] == TEXT
        block = logits[i * rows : (i + 1) * rows, :]
        loss, slope = loss_and_slope(jnp.where(is_text, block[:, :rows], block[:, rows:]))
        loss_ref[...] += jnp.where(is_text, loss, 0.0)
        text, image = jnp.where(is_text, slope, 0.0), jnp.where(is_text, 0.0, slope)
        slopes.append(jnp.concatenate([text, image], axis=1).astype(BF16))
    grads_ref[...] += by_cols(jnp.concatenate(slopes, axis=0), stack)


def first_kernel(scale, bias, roles, x_ref, y_ref, pos_ref, *rest):
    refs, (loss_ref, grads_ref, units_ref, inverses_ref, sent_ref, stack_ref) = rest[:-6], rest[-6:]
    tau, offset = scale[0], bias[0]
    rows = x_ref.shape[0]

    @pl.when(roles[len(refs)] == TEXT)
    def _():
        sent_ref[:rows, :] = y_ref[...]

    @pl.when(roles[len(refs)] != TEXT)
    def _():
        sent_ref[:rows, :] = x_ref[...]

    for i, ref in enumerate(refs, 1):
        sent_ref[i * rows : (i + 1) * rows, :] = ref[...]
    for i, ref in enumerate((x_ref, y_ref)):
        inverse = row_inverse(ref[...])
        inverses_ref[i * rows : (i + 1) * rows, :] = inverse
        units_ref[i * rows : (i + 1) * rows, :] = (ref[...].astype(F32) * inverse).astype(BF16)
    units = units_ref[...]
    x, y = units[:rows, :], units[rows:, :]
    place = lax.broadcasted_iota(jnp.int32, (rows, rows), 0)
    away = jnp.where(place == pos_ref[...], -1.0, 1.0)
    loss, slope = loss_and_slope(away * (tau * by_rows(y, x) + offset))
    slope = (slope * away).astype(BF16)
    loss_ref[...] = loss
    grads_ref[:rows, :] = by_cols(slope, y)
    grads_ref[rows:, :] = product(slope, x)
    add_blocks(roles, refs, tau, offset, units, loss_ref, grads_ref, stack_ref)


def next_kernel(scale, bias, roles, units_ref, loss_in, grads_in, *rest):
    refs, (loss_ref, grads_ref, stack_ref) = rest[:-3], rest[-3:]
    loss_ref[...] = loss_in[...]
    grads_ref[...] = grads_in[...]
    add_blocks(roles, refs, scale[0], bias[0], units_ref[...], loss_ref, grads_ref, stack_ref)


def last_kernel(
    scale, bias, odd, x_ref, y_ref, one_ref, two_ref, units_ref, inverses_ref, loss_in, grads_in, loss_ref, ix_ref, ty_ref
):
    tau, offset = scale[0], bias[0]
    rows = x_ref.shape[0]
    one, two = one_ref[...].astype(F32), two_ref[...].astype(F32)
    text, image = jnp.where(odd[0] == 1, one, two), jnp.where(odd[0] == 1, two, one)
    for i, (feats_ref, other, out_ref) in enumerate(((x_ref, text, ix_ref), (y_ref, image, ty_ref))):
        own = slice(i * rows, (i + 1) * rows)
        other = unit_rows(other)
        loss, slope = loss_and_slope(tau * by_rows(other, units_ref[own, :]) + offset)
        if i == TEXT:
            loss_ref[...] = jnp.sum(loss_in[...] + loss, axis=0, keepdims=True) / F32((SPAN + 1) * rows)
        grad = (grads_in[own, :] + by_cols(slope.astype(BF16), other)) * tau
        inverse = inverses_ref[own, :]
        norm = feats_ref[...].astype(F32) * inverse
        out_ref[...] = (grad - norm * jnp.sum(norm * grad, axis=-1, keepdims=True)) * inverse


def call(kernel, outs, blocks, scalars, *args, scratch=()):
    flops = blocks * 4 * 128 * 128 * 1152
    return pl.pallas_call(
        kernel,
        out_shape=[jax.ShapeDtypeStruct(shape, kind) for shape, kind in outs],
        in_specs=[pl.BlockSpec(memory_space=pltpu.SMEM)] * len(scalars)
        + [pl.BlockSpec(memory_space=pltpu.VMEM)] * len(args),
        out_specs=[pl.BlockSpec(memory_space=pltpu.VMEM)] * len(outs),
        scratch_shapes=scratch,
        compiler_params=pltpu.CompilerParams(vmem_limit_bytes=40 * 1024 * 1024),
        cost_estimate=pl.CostEstimate(flops=flops, bytes_accessed=blocks * 1024 * 1024, transcendentals=0),
    )(*scalars, *args)


def local(image_feats, text_feats, positive, scale, bias):
    x, y = image_feats, text_feats
    rows, width = x.shape
    index = lax.axis_index("blk")
    place = index % SPAN
    chip, core = place // CORES, place % CORES
    last = lax.axis_size("blk") - SPAN
    length = lax.axis_size("blk") // SPAN
    shifts = range(1, CHIPS)
    wrapped = around(jnp.where(index >= last, y, x))
    y_back = along_ring(y, 1)
    x_next = along_ring(x, -1)
    first = [jnp.where(chip + by < CHIPS, y, x) for by in shifts]
    near, far = in_row(first[0], 1), in_row(first[2], 3)
    first[1], near = lax.optimization_barrier((first[1], near))
    middle = in_row(first[1], 2)
    odd = index // SPAN % 2
    y_back, x_next, wrapped = lax.optimization_barrier((y_back, x_next, wrapped))
    one = swapped_along_ring(jnp.where(odd == 0, y_back, x_next), length - 1, 0)
    two = swapped_along_ring(jnp.where(odd == 1, y_back, x_next), length - 1, 1)
    double = 2 * rows
    loss_out, grads_out = ((rows, rows), F32), ((double, width), F32)
    units_out, inverses_out = ((double, width), BF16), ((double, 1), F32)
    sent_out = ((CHIPS * rows, width), BF16)
    near_role, middle_role, far_role = [(chip < by).astype(jnp.int32) for by in shifts]
    twin_role = 1 - core

    def stack(blocks):
        return [pltpu.VMEM((blocks * rows, width), BF16)]

    def more(roles, refs, units, loss, grads):
        return call(
            next_kernel, [loss_out, grads_out], len(roles), (scale, bias, jnp.stack(roles)),
            units, loss, grads, *refs, scratch=stack(len(roles)),
        )

    def inner(_):
        text = jnp.where(index < SPAN, wrapped, y_back)
        image = jnp.where(index >= last, wrapped, x_next)
        then = [jnp.where(chip + by < CHIPS, image, text) for by in shifts]
        got_roles = [near_role, middle_role, far_role]
        loss, grads, units, inverses, sent = call(
            first_kernel, [loss_out, grads_out, units_out, inverses_out, sent_out], 4,
            (scale, bias, jnp.stack(got_roles + [core])), x, y, positive, near, middle, far, scratch=stack(3),
        )
        later = [in_row(block, by) for by, block in zip(shifts, then)]
        *later, sent = lax.optimization_barrier((*later, sent))
        twin = to_twin(sent)
        later_twin = to_twin(jnp.concatenate([jnp.where(core == 0, image, text)] + later, axis=0))
        later_roles = [1 - role for role in got_roles]
        loss, grads = more([twin_role] + got_roles, [twin], units, loss, grads)
        loss, grads = more(
            later_roles + [1 - twin_role] + later_roles, later + [later_twin], units, loss, grads
        )
        return loss, grads, units, inverses

    def skip(_):
        return tuple(jnp.zeros(*out) for out in (loss_out, grads_out, units_out, inverses_out))

    go = lax.optimization_barrier(jnp.int32(1))
    loss, grads, units, inverses = lax.cond(go > 0, inner, skip, 0)
    block = ((rows, width), F32)
    loss, image_grad, text_grad = call(
        last_kernel, [((1, rows), F32), block, block], 2, (scale, bias, odd[None]),
        x, y, one, two, units, inverses, loss, grads,
    )
    return (loss[0], image_grad, text_grad)


def solution(mesh):
    rows = P(("blk", "group"), None)
    return jax.shard_map(
        local,
        mesh=mesh,
        in_specs=(rows, rows, rows, P(), P()),
        out_specs=(P(("blk", "group")), rows, rows),
        check_vma=False,
    )
```

```python
import functools

import jax
import jax.numpy as jnp
from jax import lax
from jax.experimental import pallas as pl
from jax.experimental.pallas import tpu as pltpu
from jax.sharding import PartitionSpec as P

SPAN = 8
CORES = 2
CHIPS = SPAN // CORES
F32 = jnp.float32
BF16 = jnp.bfloat16


def along_ring(x, by):
    blks, groups = lax.axis_size("blk"), lax.axis_size("group")
    length = blks // SPAN
    pairs = []
    for blk in range(blks):
        row, place = divmod(blk, SPAN)
        for group in range(groups):
            to = (group * length + row + by) % (groups * length)
            to_blk, to_group = to % length * SPAN + place, to // length
            pairs.append((blk * groups + group, to_blk * groups + to_group))
    return lax.ppermute(x, ("blk", "group"), pairs)


def swapped_along_ring(x, by, odd):
    blks, groups = lax.axis_size("blk"), lax.axis_size("group")
    length = blks // SPAN
    pairs = []
    for blk in range(blks):
        row, place = divmod(blk, SPAN)
        for group in range(groups):
            way = by if row % 2 == odd else -by
            to = (group * length + row + way) % (groups * length)
            to_blk, to_group = to % length * SPAN + place, to // length
            pairs.append((blk * groups + group, to_blk * groups + to_group))
    return lax.ppermute(x, ("blk", "group"), pairs)


def in_row(x, by):
    pairs = []
    for i in range(lax.axis_size("blk")):
        first, place = i - i % SPAN, i % SPAN
        pairs.append((i, first + (place + CORES * by) % SPAN))
    return lax.ppermute(x, "blk", pairs)


def around(x):
    last = lax.axis_size("blk") - SPAN
    pairs = [(last + i, i) for i in range(SPAN)] + [(i, last + i) for i in range(SPAN)]
    return lax.ppermute(x, "blk", pairs)


def to_twin(x):
    return lax.ppermute(x, "blk", [(i, i ^ 1) for i in range(lax.axis_size("blk"))])


def row_inverse(values):
    floats = values.astype(F32)
    return lax.rsqrt(jnp.sum(floats * floats, axis=-1, keepdims=True) + 1e-06)


def unit_rows(values):
    return (values.astype(F32) * row_inverse(values)).astype(BF16)


def by_rows(left, right):
    return lax.dot_general(left, right, (((1,), (1,)), ((), ())), preferred_element_type=F32)


def by_cols(left, right):
    return lax.dot_general(left, right, (((0,), (0,)), ((), ())), preferred_element_type=F32)


def product(left, right):
    return jnp.dot(left, right, preferred_element_type=F32)


def loss_and_slope(u):
    small = jnp.exp(-jnp.abs(u))
    whole = 1.0 + small
    return (
        jnp.maximum(u, 0.0) + jnp.log1p(small),
        jnp.where(u >= 0.0, 1.0, small) / whole,
    )


TEXT, IMAGE = 0, 1


def add_blocks(roles, refs, tau, offset, units, loss_ref, grads_ref, stack_ref):
    rows = units.shape[0] // 2
    at = 0
    for ref in refs:
        for first in range(0, ref.shape[0], rows):
            stack_ref[at : at + rows, :] = unit_rows(ref[first : first + rows, :])
            at += rows
    stack = stack_ref[...]
    logits = tau * by_rows(stack, units) + offset
    slopes = []
    for i in range(at // rows):
        is_text = roles[i] == TEXT
        block = logits[i * rows : (i + 1) * rows, :]
        loss, slope = loss_and_slope(jnp.where(is_text, block[:, :rows], block[:, rows:]))
        loss_ref[...] += jnp.where(is_text, loss, 0.0)
        text, image = jnp.where(is_text, slope, 0.0), jnp.where(is_text, 0.0, slope)
        slopes.append(jnp.concatenate([text, image], axis=1).astype(BF16))
    grads_ref[...] += by_cols(jnp.concatenate(slopes, axis=0), stack)


def first_kernel(scale, bias, roles, x_ref, y_ref, pos_ref, *rest):
    refs, (loss_ref, grads_ref, units_ref, inverses_ref, stack_ref) = rest[:-5], rest[-5:]
    tau, offset = scale[0], bias[0]
    rows = x_ref.shape[0]
    for i, ref in enumerate((x_ref, y_ref)):
        inverse = row_inverse(ref[...])
        inverses_ref[i * rows : (i + 1) * rows, :] = inverse
        units_ref[i * rows : (i + 1) * rows, :] = (ref[...].astype(F32) * inverse).astype(BF16)
    units = units_ref[...]
    x, y = units[:rows, :], units[rows:, :]
    place = lax.broadcasted_iota(jnp.int32, (rows, rows), 0)
    away = jnp.where(place == pos_ref[...], -1.0, 1.0)
    loss, slope = loss_and_slope(away * (tau * by_rows(y, x) + offset))
    slope = (slope * away).astype(BF16)
    loss_ref[...] = loss
    grads_ref[:rows, :] = by_cols(slope, y)
    grads_ref[rows:, :] = product(slope, x)
    add_blocks(roles, refs, tau, offset, units, loss_ref, grads_ref, stack_ref)


def next_kernel(scale, bias, roles, units_ref, loss_in, grads_in, *rest):
    refs, (loss_ref, grads_ref, stack_ref) = rest[:-3], rest[-3:]
    loss_ref[...] = loss_in[...]
    grads_ref[...] = grads_in[...]
    add_blocks(roles, refs, scale[0], bias[0], units_ref[...], loss_ref, grads_ref, stack_ref)


def last_kernel(
    scale, bias, odd, x_ref, y_ref, one_ref, two_ref, units_ref, inverses_ref, loss_in, grads_in, loss_ref, ix_ref, ty_ref
):
    tau, offset = scale[0], bias[0]
    rows = x_ref.shape[0]

    def finish(text_ref, image_ref):
        for i, (feats_ref, other_ref, out_ref) in enumerate(((x_ref, text_ref, ix_ref), (y_ref, image_ref, ty_ref))):
            own = slice(i * rows, (i + 1) * rows)
            other = unit_rows(other_ref[...])
            loss, slope = loss_and_slope(tau * by_rows(other, units_ref[own, :]) + offset)
            if i == TEXT:
                loss_ref[...] = jnp.sum(loss_in[...] + loss, axis=0, keepdims=True) / F32((SPAN + 1) * rows)
            grad = (grads_in[own, :] + by_cols(slope.astype(BF16), other)) * tau
            inverse = inverses_ref[own, :]
            norm = feats_ref[...].astype(F32) * inverse
            out_ref[...] = (grad - norm * jnp.sum(norm * grad, axis=-1, keepdims=True)) * inverse

    @pl.when(odd[0] == 1)
    def _():
        finish(one_ref, two_ref)

    @pl.when(odd[0] != 1)
    def _():
        finish(two_ref, one_ref)


def call(kernel, outs, blocks, scalars, *args, scratch=()):
    flops = blocks * 4 * 128 * 128 * 1152
    return pl.pallas_call(
        kernel,
        out_shape=[jax.ShapeDtypeStruct(shape, kind) for shape, kind in outs],
        in_specs=[pl.BlockSpec(memory_space=pltpu.SMEM)] * len(scalars)
        + [pl.BlockSpec(memory_space=pltpu.VMEM)] * len(args),
        out_specs=[pl.BlockSpec(memory_space=pltpu.VMEM)] * len(outs),
        scratch_shapes=scratch,
        compiler_params=pltpu.CompilerParams(vmem_limit_bytes=40 * 1024 * 1024),
        cost_estimate=pl.CostEstimate(flops=flops, bytes_accessed=blocks * 1024 * 1024, transcendentals=0),
    )(*scalars, *args)


def local(image_feats, text_feats, positive, scale, bias):
    x, y = image_feats, text_feats
    rows, width = x.shape
    index = lax.axis_index("blk")
    place = index % SPAN
    chip, core = place // CORES, place % CORES
    last = lax.axis_size("blk") - SPAN
    length = lax.axis_size("blk") // SPAN
    shifts = range(1, CHIPS)
    wrapped = around(jnp.where(index >= last, y, x))
    y_back = along_ring(y, 1)
    x_next = along_ring(x, -1)
    first = [jnp.where(chip + by < CHIPS, y, x) for by in shifts]
    near = in_row(first[0], 1)
    first[1], first[2], near = lax.optimization_barrier((first[1], first[2], near))
    middle, far = in_row(first[1], 2), in_row(first[2], 3)
    odd = index // SPAN % 2
    one = swapped_along_ring(jnp.where(odd == 0, y_back, x_next), length - 1, 0)
    two = swapped_along_ring(jnp.where(odd == 1, y_back, x_next), length - 1, 1)
    double = 2 * rows
    loss_out, grads_out = ((rows, rows), F32), ((double, width), F32)
    units_out, inverses_out = ((double, width), BF16), ((double, 1), F32)
    near_role, middle_role, far_role = [(chip < by).astype(jnp.int32) for by in shifts]
    twin_role = 1 - core

    def stack(blocks):
        return [pltpu.VMEM((blocks * rows, width), BF16)]

    def more(roles, refs, units, loss, grads):
        return call(
            next_kernel, [loss_out, grads_out], len(roles), (scale, bias, jnp.stack(roles)),
            units, loss, grads, *refs, scratch=stack(len(roles)),
        )

    def inner(_):
        text = jnp.where(index < SPAN, wrapped, y_back)
        image = jnp.where(index >= last, wrapped, x_next)
        then = [jnp.where(chip + by < CHIPS, image, text) for by in shifts]
        got, roles = [near, middle, far], [near_role, middle_role, far_role]
        twin = to_twin(jnp.concatenate([jnp.where(core == 0, y, x)] + got, axis=0))
        then[2], twin = lax.optimization_barrier((then[2], twin))
        later = [in_row(block, by) for by, block in zip(shifts, then)]
        loss, grads, units, inverses = call(
            first_kernel, [loss_out, grads_out, units_out, inverses_out], 8,
            (scale, bias, jnp.stack(roles + [twin_role] + roles)), x, y, positive, *got, twin, scratch=stack(7),
        )
        *later, loss = lax.optimization_barrier((*later, loss))
        twin = to_twin(jnp.concatenate([jnp.where(core == 0, image, text)] + later, axis=0))
        roles = [1 - role for role in roles]
        loss, grads = more(roles, later, units, loss, grads)
        loss, grads = more([1 - twin_role] + roles, [twin], units, loss, grads)
        return loss, grads, units, inverses

    def skip(_):
        return tuple(jnp.zeros(*out) for out in (loss_out, grads_out, units_out, inverses_out))

    go = lax.optimization_barrier(jnp.int32(1))
    loss, grads, units, inverses = lax.cond(go > 0, inner, skip, 0)
    block = ((rows, width), F32)
    loss, image_grad, text_grad = call(
        last_kernel, [((1, rows), F32), block, block], 2, (scale, bias, odd[None]),
        x, y, one, two, units, inverses, loss, grads,
    )
    return (loss[0], image_grad, text_grad)


def solution(mesh):
    rows = P(("blk", "group"), None)
    return jax.shard_map(
        local,
        mesh=mesh,
        in_specs=(rows, rows, rows, P(), P()),
        out_specs=(P(("blk", "group")), rows, rows),
        check_vma=False,
    )
```

```python
import functools

import jax
import jax.numpy as jnp
from jax import lax
from jax.experimental import pallas as pl
from jax.experimental.pallas import tpu as pltpu
from jax.sharding import PartitionSpec as P

SPAN = 8
CORES = 2
CHIPS = SPAN // CORES
F32 = jnp.float32
BF16 = jnp.bfloat16


def along_ring(x, by):
    blks, groups = lax.axis_size("blk"), lax.axis_size("group")
    length = blks // SPAN
    pairs = []
    for blk in range(blks):
        row, place = divmod(blk, SPAN)
        for group in range(groups):
            to = (group * length + row + by) % (groups * length)
            to_blk, to_group = to % length * SPAN + place, to // length
            pairs.append((blk * groups + group, to_blk * groups + to_group))
    return lax.ppermute(x, ("blk", "group"), pairs)


def in_row(x, by):
    pairs = []
    for i in range(lax.axis_size("blk")):
        first, place = i - i % SPAN, i % SPAN
        pairs.append((i, first + (place + CORES * by) % SPAN))
    return lax.ppermute(x, "blk", pairs)


def around(x):
    last = lax.axis_size("blk") - SPAN
    pairs = [(last + i, i) for i in range(SPAN)] + [(i, last + i) for i in range(SPAN)]
    return lax.ppermute(x, "blk", pairs)


def to_twin(x):
    return lax.ppermute(x, "blk", [(i, i ^ 1) for i in range(lax.axis_size("blk"))])


def row_inverse(values):
    floats = values.astype(F32)
    return lax.rsqrt(jnp.sum(floats * floats, axis=-1, keepdims=True) + 1e-06)


def unit_rows(values):
    return (values.astype(F32) * row_inverse(values)).astype(BF16)


def by_rows(left, right):
    return lax.dot_general(left, right, (((1,), (1,)), ((), ())), preferred_element_type=F32)


def by_cols(left, right):
    return lax.dot_general(left, right, (((0,), (0,)), ((), ())), preferred_element_type=F32)


def product(left, right):
    return jnp.dot(left, right, preferred_element_type=F32)


def loss_and_slope(u):
    small = jnp.exp(-jnp.abs(u))
    whole = 1.0 + small
    return (
        jnp.maximum(u, 0.0) + jnp.log1p(small),
        jnp.where(u >= 0.0, 1.0, small) / whole,
    )


TEXT, IMAGE = 0, 1


def add_blocks(roles, refs, tau, offset, units, loss_ref, grads_ref, stack_ref):
    rows = units.shape[0] // 2
    at = 0
    for ref in refs:
        for first in range(0, ref.shape[0], rows):
            stack_ref[at : at + rows, :] = unit_rows(ref[first : first + rows, :])
            at += rows
    stack = stack_ref[...]
    logits = tau * by_rows(stack, units) + offset
    slopes = []
    for i in range(at // rows):
        is_text = roles[i] == TEXT
        block = logits[i * rows : (i + 1) * rows, :]
        loss, slope = loss_and_slope(jnp.where(is_text, block[:, :rows], block[:, rows:]))
        loss_ref[...] += jnp.where(is_text, loss, 0.0)
        text, image = jnp.where(is_text, slope, 0.0), jnp.where(is_text, 0.0, slope)
        slopes.append(jnp.concatenate([text, image], axis=1).astype(BF16))
    grads_ref[...] += by_cols(jnp.concatenate(slopes, axis=0), stack)


def first_kernel(scale, bias, roles, x_ref, y_ref, pos_ref, *rest):
    refs, (loss_ref, grads_ref, units_ref, inverses_ref, stack_ref) = rest[:-5], rest[-5:]
    tau, offset = scale[0], bias[0]
    rows = x_ref.shape[0]
    for i, ref in enumerate((x_ref, y_ref)):
        inverse = row_inverse(ref[...])
        inverses_ref[i * rows : (i + 1) * rows, :] = inverse
        units_ref[i * rows : (i + 1) * rows, :] = (ref[...].astype(F32) * inverse).astype(BF16)
    units = units_ref[...]
    x, y = units[:rows, :], units[rows:, :]
    place = lax.broadcasted_iota(jnp.int32, (rows, rows), 0)
    away = jnp.where(place == pos_ref[...], -1.0, 1.0)
    loss, slope = loss_and_slope(away * (tau * by_rows(y, x) + offset))
    slope = (slope * away).astype(BF16)
    loss_ref[...] = loss
    grads_ref[:rows, :] = by_cols(slope, y)
    grads_ref[rows:, :] = product(slope, x)
    add_blocks([roles[i] for i in range(2 * CHIPS - 1)], refs, tau, offset, units, loss_ref, grads_ref, stack_ref)


def next_kernel(first, scale, bias, roles, units_ref, loss_in, grads_in, *rest):
    refs, (loss_ref, grads_ref, stack_ref) = rest[:-3], rest[-3:]
    loss_ref[...] = loss_in[...]
    grads_ref[...] = grads_in[...]
    count = stack_ref.shape[0] * 2 // units_ref.shape[0]
    flipped = [1 - roles[first + i] for i in range(count)]
    add_blocks(flipped, refs, scale[0], bias[0], units_ref[...], loss_ref, grads_ref, stack_ref)


def last_kernel(
    scale, bias, x_ref, y_ref, yg_ref, xg_ref, units_ref, inverses_ref, loss_in, grads_in, loss_ref, ix_ref, ty_ref
):
    tau, offset = scale[0], bias[0]
    rows = x_ref.shape[0]
    for i, (feats_ref, other_ref, out_ref) in enumerate(((x_ref, yg_ref, ix_ref), (y_ref, xg_ref, ty_ref))):
        own = slice(i * rows, (i + 1) * rows)
        other = unit_rows(other_ref[...])
        loss, slope = loss_and_slope(tau * by_rows(other, units_ref[own, :]) + offset)
        if i == TEXT:
            loss_ref[...] = jnp.sum(loss_in[...] + loss, axis=0, keepdims=True) / F32((SPAN + 1) * rows)
        grad = (grads_in[own, :] + by_cols(slope.astype(BF16), other)) * tau
        inverse = inverses_ref[own, :]
        norm = feats_ref[...].astype(F32) * inverse
        out_ref[...] = (grad - norm * jnp.sum(norm * grad, axis=-1, keepdims=True)) * inverse


def call(kernel, outs, blocks, scalars, *args, scratch=()):
    flops = blocks * 4 * 128 * 128 * 1152
    return pl.pallas_call(
        kernel,
        out_shape=[jax.ShapeDtypeStruct(shape, kind) for shape, kind in outs],
        in_specs=[pl.BlockSpec(memory_space=pltpu.SMEM)] * len(scalars)
        + [pl.BlockSpec(memory_space=pltpu.VMEM)] * len(args),
        out_specs=[pl.BlockSpec(memory_space=pltpu.VMEM)] * len(outs),
        scratch_shapes=scratch,
        compiler_params=pltpu.CompilerParams(vmem_limit_bytes=40 * 1024 * 1024),
        cost_estimate=pl.CostEstimate(flops=flops, bytes_accessed=blocks * 1024 * 1024, transcendentals=0),
    )(*scalars, *args)


def local(image_feats, text_feats, positive, scale, bias):
    x, y = image_feats, text_feats
    rows, width = x.shape
    index = lax.axis_index("blk")
    place = index % SPAN
    chip, core = place // CORES, place % CORES
    last = lax.axis_size("blk") - SPAN
    length = lax.axis_size("blk") // SPAN
    shifts = range(1, CHIPS)
    wrapped = around(jnp.where(index >= last, y, x))
    y_back = along_ring(y, 1)
    x_next = along_ring(x, -1)
    first = [jnp.where(chip + by < CHIPS, y, x) for by in shifts]
    near = in_row(first[0], 1)
    first[1], first[2], near = lax.optimization_barrier((first[1], first[2], near))
    middle, far = in_row(first[1], 2), in_row(first[2], 3)
    y_outer = along_ring(y_back, length - 1)
    x_outer = along_ring(x_next, 1 - length)
    double = 2 * rows
    loss_out, grads_out = ((rows, rows), F32), ((double, width), F32)
    units_out, inverses_out = ((double, width), BF16), ((double, 1), F32)
    near_role, middle_role, far_role = [(chip < by).astype(jnp.int32) for by in shifts]
    roles = jnp.stack([near_role, middle_role, far_role, 1 - core, near_role, middle_role, far_role])

    def stack(blocks):
        return [pltpu.VMEM((blocks * rows, width), BF16)]

    def more(first, count, refs, units, loss, grads):
        return call(
            functools.partial(next_kernel, first), [loss_out, grads_out], count, (scale, bias, roles),
            units, loss, grads, *refs, scratch=stack(count),
        )

    def inner(_):
        text = jnp.where(index < SPAN, wrapped, y_back)
        image = jnp.where(index >= last, wrapped, x_next)
        then = [jnp.where(chip + by < CHIPS, image, text) for by in shifts]
        got = [near, middle, far]
        twin = to_twin(jnp.concatenate([jnp.where(core == 0, y, x)] + got, axis=0))
        then[2], twin = lax.optimization_barrier((then[2], twin))
        later = [in_row(block, by) for by, block in zip(shifts, then)]
        loss, grads, units, inverses = call(
            first_kernel, [loss_out, grads_out, units_out, inverses_out], 8,
            (scale, bias, roles), x, y, positive, *got, twin, scratch=stack(2 * CHIPS - 1),
        )
        *later, loss = lax.optimization_barrier((*later, loss))
        twin = to_twin(jnp.concatenate([jnp.where(core == 0, image, text)] + later, axis=0))
        loss, grads = more(0, len(later), later, units, loss, grads)
        loss, grads = more(len(later), CHIPS, [twin], units, loss, grads)
        return loss, grads, units, inverses

    def skip(_):
        return tuple(jnp.zeros(*out) for out in (loss_out, grads_out, units_out, inverses_out))

    go = lax.optimization_barrier(jnp.int32(1))
    loss, grads, units, inverses = lax.cond(go > 0, inner, skip, 0)
    block = ((rows, width), F32)
    loss, image_grad, text_grad = call(
        last_kernel, [((1, rows), F32), block, block], 2, (scale, bias),
        x, y, y_outer, x_outer, units, inverses, loss, grads,
    )
    return (loss[0], image_grad, text_grad)


def solution(mesh):
    rows = P(("blk", "group"), None)
    return jax.shard_map(
        local,
        mesh=mesh,
        in_specs=(rows, rows, rows, P(), P()),
        out_specs=(P(("blk", "group")), rows, rows),
        check_vma=False,
    )
```

```python
import functools

import jax
import jax.numpy as jnp
from jax import lax
from jax.experimental import pallas as pl
from jax.experimental.pallas import tpu as pltpu
from jax.sharding import PartitionSpec as P

SPAN = 8
CORES = 2
CHIPS = SPAN // CORES
F32 = jnp.float32
BF16 = jnp.bfloat16


def along_ring(x, by):
    blks, groups = lax.axis_size("blk"), lax.axis_size("group")
    length = blks // SPAN
    pairs = []
    for blk in range(blks):
        row, place = divmod(blk, SPAN)
        for group in range(groups):
            to = (group * length + row + by) % (groups * length)
            to_blk, to_group = to % length * SPAN + place, to // length
            pairs.append((blk * groups + group, to_blk * groups + to_group))
    return lax.ppermute(x, ("blk", "group"), pairs)


def in_row(x, by):
    pairs = []
    for i in range(lax.axis_size("blk")):
        first, place = i - i % SPAN, i % SPAN
        pairs.append((i, first + (place + CORES * by) % SPAN))
    return lax.ppermute(x, "blk", pairs)


def around(x):
    last = lax.axis_size("blk") - SPAN
    pairs = [(last + i, i) for i in range(SPAN)] + [(i, last + i) for i in range(SPAN)]
    return lax.ppermute(x, "blk", pairs)


def to_twin(x):
    return lax.ppermute(x, "blk", [(i, i ^ 1) for i in range(lax.axis_size("blk"))])


def row_inverse(values):
    floats = values.astype(F32)
    return lax.rsqrt(jnp.sum(floats * floats, axis=-1, keepdims=True) + 1e-06)


def unit_rows(values):
    return (values.astype(F32) * row_inverse(values)).astype(BF16)


def by_rows(left, right):
    return lax.dot_general(left, right, (((1,), (1,)), ((), ())), preferred_element_type=F32)


def by_cols(left, right):
    return lax.dot_general(left, right, (((0,), (0,)), ((), ())), preferred_element_type=F32)


def product(left, right):
    return jnp.dot(left, right, preferred_element_type=F32)


def loss_and_slope(u):
    small = jnp.exp(-jnp.abs(u))
    whole = 1.0 + small
    return (
        jnp.maximum(u, 0.0) + jnp.log1p(small),
        jnp.where(u >= 0.0, 1.0, small) / whole,
    )


TEXT, IMAGE = 0, 1


def add_blocks(roles, refs, tau, offset, units, loss_ref, grads_ref, stack_ref):
    rows = units.shape[0] // 2
    at = 0
    for ref in refs:
        for first in range(0, ref.shape[0], rows):
            stack_ref[at : at + rows, :] = unit_rows(ref[first : first + rows, :])
            at += rows
    stack = stack_ref[...]
    logits = tau * by_rows(stack, units) + offset
    slopes = []
    for i in range(at // rows):
        is_text = roles[i] == TEXT
        block = logits[i * rows : (i + 1) * rows, :]
        loss, slope = loss_and_slope(jnp.where(is_text, block[:, :rows], block[:, rows:]))
        loss_ref[...] += jnp.where(is_text, loss, 0.0)
        text, image = jnp.where(is_text, slope, 0.0), jnp.where(is_text, 0.0, slope)
        slopes.append(jnp.concatenate([text, image], axis=1).astype(BF16))
    grads_ref[...] += by_cols(jnp.concatenate(slopes, axis=0), stack)


def first_kernel(scale, bias, roles, x_ref, y_ref, pos_ref, *rest):
    refs, (loss_ref, grads_ref, units_ref, inverses_ref, stack_ref) = rest[:-5], rest[-5:]
    tau, offset = scale[0], bias[0]
    rows = x_ref.shape[0]
    for i, ref in enumerate((x_ref, y_ref)):
        inverse = row_inverse(ref[...])
        inverses_ref[i * rows : (i + 1) * rows, :] = inverse
        units_ref[i * rows : (i + 1) * rows, :] = (ref[...].astype(F32) * inverse).astype(BF16)
    units = units_ref[...]
    x, y = units[:rows, :], units[rows:, :]
    place = lax.broadcasted_iota(jnp.int32, (rows, rows), 0)
    away = jnp.where(place == pos_ref[...], -1.0, 1.0)
    loss, slope = loss_and_slope(away * (tau * by_rows(y, x) + offset))
    slope = (slope * away).astype(BF16)
    loss_ref[...] = loss
    grads_ref[:rows, :] = by_cols(slope, y)
    grads_ref[rows:, :] = product(slope, x)
    count = stack_ref.shape[0] // rows
    add_blocks([roles[i] for i in range(count)], refs, tau, offset, units, loss_ref, grads_ref, stack_ref)


def next_kernel(first, scale, bias, roles, units_ref, loss_in, grads_in, *rest):
    refs, (loss_ref, grads_ref, stack_ref) = rest[:-3], rest[-3:]
    loss_ref[...] = loss_in[...]
    grads_ref[...] = grads_in[...]
    count = stack_ref.shape[0] * 2 // units_ref.shape[0]
    add_blocks([roles[first + i] for i in range(count)], refs, scale[0], bias[0], units_ref[...], loss_ref, grads_ref, stack_ref)


def outer_grad(tau, offset, feats_ref, other_ref, unit, inverse, before):
    other = unit_rows(other_ref[...])
    loss, slope = loss_and_slope(tau * by_rows(other, unit) + offset)
    grad = (before + by_cols(slope.astype(BF16), other)) * tau
    norm = feats_ref[...].astype(F32) * inverse
    return loss, (grad - norm * jnp.sum(norm * grad, axis=-1, keepdims=True)) * inverse


def image_kernel(scale, bias, x_ref, other_ref, units_ref, inverses_ref, loss_in, grads_in, loss_ref, out_ref):
    rows = x_ref.shape[0]
    own = slice(0, rows)
    loss, out_ref[...] = outer_grad(
        scale[0], bias[0], x_ref, other_ref, units_ref[own, :], inverses_ref[own, :], grads_in[own, :]
    )
    loss_ref[...] = jnp.sum(loss_in[...] + loss, axis=0, keepdims=True) / F32((SPAN + 1) * rows)


def text_kernel(scale, bias, y_ref, other_ref, units_ref, inverses_ref, grads_in, out_ref):
    rows = y_ref.shape[0]
    own = slice(rows, 2 * rows)
    _, out_ref[...] = outer_grad(
        scale[0], bias[0], y_ref, other_ref, units_ref[own, :], inverses_ref[own, :], grads_in[own, :]
    )


def call(kernel, outs, blocks, scalars, *args, scratch=()):
    flops = blocks * 4 * 128 * 128 * 1152
    return pl.pallas_call(
        kernel,
        out_shape=[jax.ShapeDtypeStruct(shape, kind) for shape, kind in outs],
        in_specs=[pl.BlockSpec(memory_space=pltpu.SMEM)] * len(scalars)
        + [pl.BlockSpec(memory_space=pltpu.VMEM)] * len(args),
        out_specs=[pl.BlockSpec(memory_space=pltpu.VMEM)] * len(outs),
        scratch_shapes=scratch,
        compiler_params=pltpu.CompilerParams(vmem_limit_bytes=40 * 1024 * 1024),
        cost_estimate=pl.CostEstimate(flops=flops, bytes_accessed=blocks * 1024 * 1024, transcendentals=0),
    )(*scalars, *args)


def local(image_feats, text_feats, positive, scale, bias):
    x, y = image_feats, text_feats
    rows, width = x.shape
    index = lax.axis_index("blk")
    place = index % SPAN
    chip, core = place // CORES, place % CORES
    last = lax.axis_size("blk") - SPAN
    length = lax.axis_size("blk") // SPAN
    shifts = range(1, CHIPS)
    wrapped = around(jnp.where(index >= last, y, x))
    y_back = along_ring(y, 1)
    x_next = along_ring(x, -1)
    first = [jnp.where(chip + by < CHIPS, y, x) for by in shifts]
    near, far = in_row(first[0], 1), in_row(first[2], 3)
    y_outer = along_ring(y_back, length - 1)
    x_outer = along_ring(x_next, 1 - length)
    double = 2 * rows
    loss_out, grads_out = ((rows, rows), F32), ((double, width), F32)
    units_out, inverses_out = ((double, width), BF16), ((double, 1), F32)
    near_role, middle_role, far_role = [(chip < by).astype(jnp.int32) for by in shifts]
    early = [near_role, far_role, 1 - core, near_role, far_role]
    late = [middle_role, 1 - middle_role, 1 - near_role, 1 - far_role, core]
    roles = jnp.stack(early + late + late[:-1])

    def stack(blocks):
        return [pltpu.VMEM((blocks * rows, width), BF16)]

    def more(first, count, refs, units, loss, grads):
        return call(
            functools.partial(next_kernel, first), [loss_out, grads_out], count, (scale, bias, roles),
            units, loss, grads, *refs, scratch=stack(count),
        )

    def inner(_):
        text = jnp.where(index < SPAN, wrapped, y_back)
        image = jnp.where(index >= last, wrapped, x_next)
        then = [jnp.where(chip + by < CHIPS, image, text) for by in shifts]
        twin = to_twin(jnp.concatenate([jnp.where(core == 0, y, x), near, far], axis=0))
        then[2], twin = lax.optimization_barrier((then[2], twin))
        later = [in_row(jnp.concatenate([first[1], then[1]], axis=0), 2), in_row(then[0], 1), in_row(then[2], 3)]
        loss, grads, units, inverses = call(
            first_kernel, [loss_out, grads_out, units_out, inverses_out], 6,
            (scale, bias, roles), x, y, positive, near, far, twin, scratch=stack(5),
        )
        *later, loss = lax.optimization_barrier((*later, loss))
        twin = to_twin(jnp.concatenate([jnp.where(core == 0, image, text)] + later, axis=0))
        loss, grads = more(5, 4, later, units, loss, grads)
        loss, grads = more(9, 5, [twin], units, loss, grads)
        return loss, grads, units, inverses

    def skip(_):
        return tuple(jnp.zeros(*out) for out in (loss_out, grads_out, units_out, inverses_out))

    go = lax.optimization_barrier(jnp.int32(1))
    loss, grads, units, inverses = lax.cond(go > 0, inner, skip, 0)
    block = ((rows, width), F32)
    loss, image_grad = call(
        image_kernel, [((1, rows), F32), block], 1, (scale, bias), x, y_outer, units, inverses, loss, grads
    )
    (text_grad,) = call(text_kernel, [block], 1, (scale, bias), y, x_outer, units, inverses, grads)
    return (loss[0], image_grad, text_grad)


def solution(mesh):
    rows = P(("blk", "group"), None)
    return jax.shard_map(
        local,
        mesh=mesh,
        in_specs=(rows, rows, rows, P(), P()),
        out_specs=(P(("blk", "group")), rows, rows),
        check_vma=False,
    )
```
